512 devices in a mesh: slide: 16 (over y, x_lo, core), row: 32 (over z, x_hi).
Axes of the slice: x: 4 (x_hi: 2, x_lo: 2; x = x_hi * 2 + x_lo), y: 4, z: 16, core: 2. Of those that a mesh axis runs over, the one named last changes fastest.
Arguments:
- trunk_c3: bfloat16 [16, 256, 32, 512], P('slide', 'row'), may hold values from -6 to 6
- trunk_c4: bfloat16 [16, 128, 16, 1024], P('slide', 'row'), may hold values from -6 to 6
- feat_p3: bfloat16 [16, 256, 32, 256], P('slide', 'row'), may hold values from -6 to 6
- feat_p4: bfloat16 [16, 128, 16, 256], P('slide', 'row'), may hold values from -6 to 6
- pre_p3: bfloat16 [16, 256, 32, 256], P('slide', 'row'), may hold values from -6 to 6
- pre_p4: bfloat16 [16, 128, 16, 256], P('slide', 'row'), may hold values from -6 to 6
- grad_p3: bfloat16 [16, 256, 32, 256], P('slide', 'row'), may hold values from -6 to 6
- grad_p4: bfloat16 [16, 128, 16, 256], P('slide', 'row'), may hold values from -6 to 6
- keep_p3: int32 [16, 256, 32], P('slide', 'row'), may hold values 0 or 1
- keep_p4: int32 [16, 128, 16], P('slide', 'row'), may hold values 0 or 1
- head_w: bfloat16 [9, 256, 256], replicated, may hold values from -0.125 to 0.125
- lateral_c3: bfloat16 [512, 256], replicated, may hold values from -0.25 to 0.25
- lateral_c4: bfloat16 [1024, 256], replicated, may hold values from -0.1875 to 0.1875
Outputs:
- trunk_c3_grad: bfloat16 [16, 256, 32, 512], P('slide', 'row')
- trunk_c4_grad: bfloat16 [16, 128, 16, 1024], P('slide', 'row')
- head_grad: float32 [2304, 256], P('row')
- bias_grad: float32 [256], P('row')
- lateral_c3_grad: float32 [512, 256], P('row')
- lateral_c4_grad: float32 [1024, 256], P('row')
The draws below stay inside these ranges and needn't reach their ends.
All inputs are finite; a program needn't handle non-finite values. No bound on the sum of `keep_p3` or of `keep_p4` on one device may be relied on, other than what follows from the above.
Results may differ from the reference program's by a relative error of at most 0.011.
Values may be sent and summed in bfloat16 or wider, within the bound.
A program may use at most 64 MiB of HBM per device.

```python
import jax
import jax.numpy as jnp
from jax import lax

CH = 256
C3CH = 512
C4CH = 1024
W3 = 32
SLIDES = 16
H3 = 256
H4 = 128
W4 = 16


def set_ends(values, stream_key, least, largest):
    spot = [jax.random.randint(jax.random.fold_in(stream_key, axis), (), 0, length) for axis, length in enumerate(values.shape)]
    longest = values.shape.index(max(values.shape))
    next_to = spot[:longest] + [(spot[longest] + 1) % values.shape[longest]] + spot[longest + 1:]
    return values.at[tuple(spot)].set(least).at[tuple(next_to)].set(largest)


def block_scale(key, shape, pieces, least, largest):
    level = 1.0
    for dim, blocks in pieces:
        steps = jax.random.uniform(jax.random.fold_in(jax.random.fold_in(key, 6), dim), (blocks,), jnp.float32, least / len(pieces), largest / len(pieces))
        level = level * jnp.repeat(jnp.exp(steps), shape[dim] // blocks).reshape((-1,) + (1,) * (len(shape) - 1 - dim))
    return level


def normal_values(own_key, dims, scale, limit, pieces=(), held_as=jnp.bfloat16):
    values = jax.random.normal(own_key, dims, jnp.float32) * scale
    if len(pieces) > 0:
        values = block_scale(own_key, dims, pieces, -0.22, 0.18) * values
    return jnp.clip(values, min=-limit, max=limit).astype(held_as)


def setup_inputs(seed: int = 0) -> dict:
    splits = jax.random.split(jax.random.key(seed), 14)
    trunk_c3 = normal_values(splits[0], (SLIDES, H3, W3, C3CH), 1.0, 6.0, ((0, 16), (1, 32)))
    trunk_c4 = normal_values(splits[1], (SLIDES, H4, W4, C4CH), 1.0, 6.0, ((0, 16), (1, 32)))
    feat_p3 = normal_values(splits[2], (SLIDES, H3, W3, CH), 1.0, 6.0, ((0, 16), (1, 32)))
    feat_p4 = normal_values(splits[3], (SLIDES, H4, W4, CH), 1.0, 6.0, ((0, 16), (1, 32)))
    pre_p3 = normal_values(splits[4], (SLIDES, H3, W3, CH), 1.0, 6.0, ((0, 16), (1, 32)))
    pre_p4 = normal_values(splits[5], (SLIDES, H4, W4, CH), 1.0, 6.0, ((0, 16), (1, 32)))
    grad_p3 = normal_values(splits[6], (SLIDES, H3, W3, CH), 1.0, 6.0, ((0, 16), (1, 32)))
    grad_p4 = normal_values(splits[7], (SLIDES, H4, W4, CH), 1.0, 6.0, ((0, 16), (1, 32)))
    keep_p3 = set_ends((jax.random.randint(splits[8], (SLIDES, H3, W3), 0, 4) < 3).astype(jnp.int32), jax.random.fold_in(splits[8], 1), 0, 1)
    keep_p4 = set_ends((jax.random.randint(splits[9], (SLIDES, H4, W4), 0, 4) < 3).astype(jnp.int32), jax.random.fold_in(splits[9], 1), 0, 1)
    head_w = normal_values(splits[10], (9, CH, CH), (9 * CH) ** -0.5, 0.125)
    lateral_c3 = normal_values(splits[11], (C3CH, CH), C3CH ** -0.5, 0.25)
    lateral_c4 = normal_values(splits[12], (C4CH, CH), C4CH ** -0.5, 0.1875)
    return dict(trunk_c3=trunk_c3, trunk_c4=trunk_c4, feat_p3=feat_p3, feat_p4=feat_p4, pre_p3=pre_p3, pre_p4=pre_p4, grad_p3=grad_p3, grad_p4=grad_p4, keep_p3=keep_p3, keep_p4=keep_p4, head_w=head_w, lateral_c3=lateral_c3, lateral_c4=lateral_c4)


loss_scale = 256.0


def head_level(feature, preact, cotangent, keep_mask, head_w):
    row_total, col_total, channels = feature.shape
    live = jnp.logical_and(keep_mask[..., None] == 1, preact > 0)
    delta = jnp.where(live, cotangent, jnp.zeros_like(cotangent))
    delta_pad = jnp.pad(delta, ((1, 1), (1, 1), (0, 0)))
    feat_pad = jnp.pad(feature, ((1, 1), (1, 1), (0, 0)))
    delta_flat = delta.reshape(-1, channels)
    backward = jnp.zeros((row_total * col_total, channels), jnp.float32)
    weight_terms = []
    for row_tap in range(3):
        for col_tap in range(3):
            moved = delta_pad[2 - row_tap:2 - row_tap + row_total, 2 - col_tap:2 - col_tap + col_total].reshape(-1, channels)
            backward = backward + jnp.dot(moved, head_w[3 * row_tap + col_tap].T, preferred_element_type=jnp.float32)
            window = feat_pad[row_tap:row_tap + row_total, col_tap:col_tap + col_total].reshape(-1, channels)
            weight_terms.append(jnp.dot(window.T, delta_flat, preferred_element_type=jnp.float32))
    bias_term = jnp.sum(delta_flat.astype(jnp.float32), axis=0)
    return backward.reshape(row_total, col_total, channels), jnp.stack(weight_terms), bias_term


def reference(trunk_c3, trunk_c4, feat_p3, feat_p4, pre_p3, pre_p4, grad_p3, grad_p4, keep_p3, keep_p4, head_w, lateral_c3, lateral_c4):
    channels = head_w.shape[1]

    def one_slide(slide_id):
        back_fine, wsum_fine, bsum_fine = head_level(feat_p3[slide_id], pre_p3[slide_id], grad_p3[slide_id], keep_p3[slide_id], head_w)
        back_coarse, wsum_coarse, bsum_coarse = head_level(feat_p4[slide_id], pre_p4[slide_id], grad_p4[slide_id], keep_p4[slide_id], head_w)
        fine_rows, fine_cols = back_fine.shape[0], back_fine.shape[1]
        pooled = back_fine.reshape(fine_rows // 2, 2, fine_cols // 2, 2, channels).sum(axis=(1, 3))
        lat_fine = back_fine.astype(jnp.bfloat16).reshape(-1, channels)
        lat_coarse = (back_coarse + pooled).astype(jnp.bfloat16).reshape(-1, channels)
        trunk_fine = trunk_c3[slide_id].reshape(-1, trunk_c3.shape[-1])
        trunk_coarse = trunk_c4[slide_id].reshape(-1, trunk_c4.shape[-1])
        fine_grad = jnp.dot(lat_fine, lateral_c3.T, preferred_element_type=jnp.float32).astype(jnp.bfloat16)
        coarse_grad = jnp.dot(lat_coarse, lateral_c4.T, preferred_element_type=jnp.float32).astype(jnp.bfloat16)
        fine_lateral = jnp.dot(trunk_fine.T, lat_fine, preferred_element_type=jnp.float32)
        coarse_lateral = jnp.dot(trunk_coarse.T, lat_coarse, preferred_element_type=jnp.float32)
        fine_grad = fine_grad.reshape(fine_rows, fine_cols, trunk_c3.shape[-1])
        coarse_grad = coarse_grad.reshape(fine_rows // 2, fine_cols // 2, trunk_c4.shape[-1])
        return fine_grad, coarse_grad, wsum_fine + wsum_coarse, bsum_fine + bsum_coarse, fine_lateral, coarse_lateral

    results = lax.map(one_slide, jnp.arange(trunk_c3.shape[0], dtype=jnp.int32))
    head_grad = jnp.sum(results[2], axis=0).reshape(9 * channels, channels) / loss_scale
    bias_grad = jnp.sum(results[3], axis=0) / loss_scale
    lateral_c3_grad = jnp.sum(results[4], axis=0) / loss_scale
    lateral_c4_grad = jnp.sum(results[5], axis=0) / loss_scale
    return (results[0], results[1], head_grad, bias_grad, lateral_c3_grad, lateral_c4_grad)
```

```python
import jax
import jax.numpy as jnp
from jax import lax
from jax.experimental import pallas as pl
from jax.experimental.pallas import tpu as pltpu
from jax.sharding import PartitionSpec as P

MESH = pl.DeviceIdType.MESH
F32 = jnp.float32
BF16 = jnp.bfloat16
LOSS_SCALE = 256.0

ROW_C3 = 2304
ROW_C4 = 2816
ROW_BIAS = 3840
ROWS = 3856
CORE_PARTS = ((768, 768), (0, 768), (1536, 768), (ROW_C3, 512), (ROW_C4, 1040))


def nt(a, b):
    return lax.dot_general(a, b, (((1,), (1,)), ((), ())), preferred_element_type=F32)


def nn(a, b):
    return jnp.dot(a, b, preferred_element_type=F32)


def kernel(
    tc3_h, tc4_h, f3_h, f4_h, p3_h, p4_h, g3_h, g4_h, k3_h, k4_h, hw_h, l3_h, l4_h,
    o_t3, o_t4, o_head, o_bias, o_l3, o_l4,
    tc3, tc4, f3, f4, p3, p4, g3, g4, k3, k4, hw, l3, l4,
    f3t, f4t, dx3, dx4, halo_s, halo_r, grads, core_s, core_r,
    bx, by, r1x, r1y, cx, cy, r2x, r2y, dz, r3, gath,
    in_sem, halo_ss, halo_rs, core_ss, core_rs, s1_ss, s1_rs, s2_ss, s2_rs,
    z_ss, z_rs, ag_ss, ag_rs, far_sem,
):
    slide = lax.axis_index("slide")
    row = lax.axis_index("row")
    core = lax.rem(slide, 2)
    x_lo = lax.rem(slide // 2, 2)
    y = slide // 4
    z = row // 2
    x_hi = lax.rem(row, 2)
    x = 2 * x_hi + x_lo

    def dev(xx, yy, zz, cc):
        return ((yy * 2 + lax.rem(xx, 2)) * 2 + cc, zz * 2 + xx // 2)

    sibling = (slide + 1 - 2 * core, row)
    above = (slide, lax.rem(row + 31, 32))
    below = (slide, lax.rem(row + 1, 32))
    x_dev = [dev(lax.rem(x + d, 4), y, z, core) for d in (1, 2, 3)]
    y_dev = [dev(x, lax.rem(y + d, 4), z, core) for d in (1, 2, 3)]

    def z_dev(d):
        return dev(x, y, lax.rem(z + d + 16, 16), core)

    pairs = [
        (k3_h, k3), (k4_h, k4), (p3_h, p3), (g3_h, g3), (p4_h, p4), (g4_h, g4), (f3_h, f3),
        (f4_h, f4), (hw_h, hw), (tc3_h, tc3), (tc4_h, tc4), (l3_h, l3), (l4_h, l4),
    ]
    loads = [pltpu.make_async_copy(a, b, in_sem.at[i]) for i, (a, b) in enumerate(pairs)]

    barrier = pltpu.get_barrier_semaphore()
    partners = [above, below, sibling] + x_dev + y_dev
    partners += [z_dev(d) for d in (-4, -3, -2, -1, 1, 2, 3, 4)]
    for who in partners:
        pl.semaphore_signal(barrier, inc=1, device_id=who, device_id_type=MESH)
    for ld in loads:
        ld.start()

    for ld in loads[:6]:
        ld.wait()

    def delta(keep, pre, grad, height, width):
        keep_t = jnp.transpose(keep[...].astype(F32))
        cols = [jnp.broadcast_to(keep_t[:, i : i + 1], (width, 256)) for i in range(height)]
        mask = jnp.concatenate(cols, axis=0)
        live = jnp.logical_and(mask > 0.5, pre[...].astype(F32) > 0.0)
        return jnp.where(live, grad[...].astype(F32), 0.0)

    def put_shifted(dst, start, rows, width, val):
        col = lax.rem(lax.broadcasted_iota(jnp.int32, (rows, 256), 0), width)
        ahead = jnp.where(col == width - 1, 0.0, pltpu.roll(val, rows - 1, 0))
        behind = jnp.where(col == 0, 0.0, pltpu.roll(val, 1, 0))
        dst[0, start : start + rows, :] = ahead.astype(BF16)
        dst[1, start : start + rows, :] = val.astype(BF16)
        dst[2, start : start + rows, :] = behind.astype(BF16)

    d3 = delta(k3, p3, g3, 8, 32)
    d4 = delta(k4, p4, g4, 4, 16)
    halo_s[0, 0:32, :] = d3[0:32].astype(BF16)
    halo_s[0, 32:48, :] = d4[0:16].astype(BF16)
    halo_s[1, 0:32, :] = d3[224:256].astype(BF16)
    halo_s[1, 32:48, :] = d4[48:64].astype(BF16)

    pl.semaphore_wait(barrier, len(partners))
    halos = []
    for i, who in enumerate((above, below)):
        cp = pltpu.make_async_remote_copy(
            src_ref=halo_s.at[i], dst_ref=halo_r.at[i], send_sem=halo_ss.at[i],
            recv_sem=halo_rs.at[i], device_id=who, device_id_type=MESH,
        )
        cp.start()
        halos.append(cp)
    for d in (-4, 4):
        pl.semaphore_signal(far_sem, inc=1, device_id=z_dev(d), device_id_type=MESH)

    put_shifted(dx3, 32, 256, 32, d3)
    put_shifted(dx4, 16, 64, 16, d4)

    ones = jnp.ones((16, 256), BF16)
    bias = nn(ones, dx3[1, 32:288, :]) + nn(ones[:, :64], dx4[1, 16:80, :])

    first = core == 0

    def emit(start, rows, val):
        lo, hi = val[:, :128], val[:, 128:]
        grads[start : start + rows, :] = jnp.where(first, lo, hi)
        core_s[start : start + rows, :] = jnp.where(first, hi, lo).astype(BF16)

    core_copies = []

    def send_core(i):
        start, rows = CORE_PARTS[i]
        cp = pltpu.make_async_remote_copy(
            src_ref=core_s.at[pl.ds(start, rows)], dst_ref=core_r.at[pl.ds(start, rows)],
            send_sem=core_ss.at[i], recv_sem=core_rs.at[i], device_id=sibling,
            device_id_type=MESH,
        )
        cp.start()
        core_copies.append(cp)

    emit(ROW_BIAS, 16, bias)
    loads[6].wait()
    loads[7].wait()
    f3t[...] = jnp.transpose(f3[...])
    f4t[...] = jnp.transpose(f4[...])

    def head_taps(a):
        for b in range(3):
            tap = 3 * a + b
            top3, top4 = (2 - a) * 32, (2 - a) * 16
            val = nn(f3t[...], dx3[b, top3 : top3 + 256, :])
            val = val + nn(f4t[...], dx4[b, top4 : top4 + 64, :])
            emit(tap * 256, 256, val)

    head_taps(1)
    send_core(0)
    for ld in loads[8:]:
        ld.wait()

    for cp in halos:
        cp.wait_recv()
    low = jnp.where(row < 31, halo_r[0].astype(F32), 0.0)
    top = jnp.where(row > 0, halo_r[1].astype(F32), 0.0)
    put_shifted(dx3, 0, 32, 32, top[0:32])
    put_shifted(dx3, 288, 32, 32, low[0:32])
    put_shifted(dx4, 0, 16, 16, top[32:48])
    put_shifted(dx4, 80, 16, 16, low[32:48])

    back = jnp.zeros((320, 256), F32)
    for a in range(3):
        for b in range(3):
            top3, top4 = (2 - a) * 32, (2 - a) * 16
            patch = jnp.concatenate(
                [dx3[b, top3 : top3 + 256, :], dx4[b, top4 : top4 + 64, :]], axis=0
            )
            back = back + nt(patch, hw[3 * a + b])
    back3 = back[0:256]
    back4 = back[256:320]
    lat3 = back3.astype(BF16)
    rest = (back3 - lat3.astype(F32)).astype(BF16)
    cell4 = lax.broadcasted_iota(jnp.int32, (64, 256), 0)
    cell3 = lax.broadcasted_iota(jnp.int32, (64, 256), 1)
    home = (cell3 // 64) * 16 + lax.rem(cell3, 32) // 2
    pool = jnp.where(home == cell4, 1.0, 0.0).astype(BF16)
    pooled = nn(pool, lat3) + nn(pool, rest)
    lat4 = (back4 + pooled).astype(BF16)

    head_taps(0)
    send_core(1)
    head_taps(2)
    send_core(2)
    emit(ROW_C3, 512, nn(jnp.transpose(tc3[...]), lat3))
    send_core(3)
    emit(ROW_C4, 1024, nn(jnp.transpose(tc4[...]), lat4))
    send_core(4)

    o_t3[...] = nt(lat3, l3[...]).astype(BF16)
    o_t4[...] = nt(lat4, l4[...]).astype(BF16)

    for i, (start, rows) in enumerate(CORE_PARTS):
        core_copies[i].wait_recv()
        grads[start : start + rows, :] += core_r[start : start + rows, :].astype(F32)

    def pack(dst, z_first, flip):
        def step(zz, carry):
            for xh in range(2):
                r = 2 * (zz + z_first) + xh
                base = pl.multiple_of(72 * r, 8)
                for blk in range(8):
                    if blk < 4:
                        val = grads[pl.ds(base + 16 * blk, 16), :]
                    elif blk == 4:
                        val = jnp.concatenate(
                            [grads[pl.ds(base + 64, 8), :], grads[ROW_BIAS : ROW_BIAS + 8, :]],
                            axis=0,
                        )
                    elif blk == 5:
                        val = grads[pl.ds(pl.multiple_of(ROW_C3 + 16 * r, 16), 16), :]
                    else:
                        at = ROW_C4 + 32 * r + 16 * (blk - 6)
                        val = grads[pl.ds(pl.multiple_of(at, 16), 16), :]
                    xx, yy = 2 * xh + blk % 2, blk // 2
                    if flip:
                        dst[yy, xx, zz] = val.astype(BF16)
                    else:
                        dst[xx, yy, zz] = val.astype(BF16)
            return carry

        lax.fori_loop(0, 8, step, 0)

    def exchange(src, at, dst, who, ss, rs, base):
        out = []
        for d in (2, 1, 3):
            cp = pltpu.make_async_remote_copy(
                src_ref=src.at[lax.rem(at + d, 4)], dst_ref=dst.at[d - 1],
                send_sem=ss.at[base + d - 1], recv_sem=rs.at[base + d - 1],
                device_id=who[d - 1], device_id_type=MESH,
            )
            cp.start()
            out.append(cp)
        return out

    sends = list(halos) + list(core_copies)
    pack(bx, 0, False)
    s1x = exchange(bx, x, r1x, x_dev, s1_ss, s1_rs, 0)
    pack(by, 8, True)
    s1y = exchange(by, y, r1y, y_dev, s1_ss, s1_rs, 3)

    def total(mine, got, i):
        acc = mine.astype(F32)
        for d in range(3):
            acc = acc + (got[d] if i is None else got[d, i]).astype(F32)
        return acc

    for cp in s1x:
        cp.wait_recv()
    for i in range(4):
        cx[i] = total(bx[x, i], r1x, i).astype(BF16)
    s2x = exchange(cx, y, r2x, y_dev, s2_ss, s2_rs, 0)
    for cp in s1y:
        cp.wait_recv()
    for i in range(4):
        cy[i] = total(by[y, i], r1y, i).astype(BF16)
    s2y = exchange(cy, x, r2y, x_dev, s2_ss, s2_rs, 3)

    def z_copy(piece, d):
        return pltpu.make_async_remote_copy(
            src_ref=dz.at[piece], dst_ref=r3.at[d], send_sem=z_ss.at[d], recv_sem=z_rs.at[d],
            device_id=z_dev(d), device_id_type=MESH,
        )

    def send_z(z_first):
        for piece in range(z_first, z_first + 8):
            d = lax.rem(piece - z + 16, 16)

            @pl.when(d != 0)
            def _():
                z_copy(piece, d).start()

    for cp in s2x:
        cp.wait_recv()
    dz[0:8] = total(cx[y], r2x, None).astype(BF16)
    pl.semaphore_wait(far_sem, 2)
    send_z(0)
    for cp in s2y:
        cp.wait_recv()
    dz[8:16] = total(cy[x], r2y, None).astype(BF16)
    send_z(8)

    acc = dz[z].astype(F32)
    for d in range(1, 16):
        z_copy(0, d).wait_recv()
        acc = acc + r3[d].astype(F32)

    gath[slide] = acc * (1.0 / LOSS_SCALE)
    gathers = []
    for o in range(1, 16):
        dy, dx, dc = o // 4, (o // 2) % 2, o % 2
        xl = lax.rem(x_lo + dx, 2)
        cc = lax.rem(core + dc, 2)
        cp = pltpu.make_async_remote_copy(
            src_ref=gath.at[slide], dst_ref=gath.at[slide], send_sem=ag_ss.at[o],
            recv_sem=ag_rs.at[o], device_id=dev(2 * x_hi + xl, lax.rem(y + dy, 4), z, cc),
            device_id_type=MESH,
        )
        cp.start()
        gathers.append(cp)
    for cp in gathers:
        cp.wait_recv()

    for c in range(2):
        lanes = slice(128 * c, 128 * c + 128)
        for blk in range(4):
            o_head[16 * blk : 16 * blk + 16, lanes] = gath[2 * blk + c]
        o_head[64:72, lanes] = gath[8 + c, 0:8, :]
        o_l3[:, lanes] = gath[10 + c]
        o_l4[0:16, lanes] = gath[12 + c]
        o_l4[16:32, lanes] = gath[14 + c]
    sums = jnp.concatenate([gath[8, 8:16, :], gath[9, 8:16, :]], axis=1)
    lane = lax.broadcasted_iota(jnp.int32, (8, 256), 1)
    sub = lax.broadcasted_iota(jnp.int32, (8, 256), 0)
    mine = jnp.where(lane == 8 * row + sub, sums, 0.0)
    for i in range(8):
        o_bias[i] = jnp.sum(mine[i : i + 1, :])

    for cp in sends + s1x + s1y + s2x + s2y + gathers:
        cp.wait_send()
    for d in range(1, 16):
        z_copy(0, d).wait_send()


def local(*args):
    shapes = (
        (256, 512), (64, 1024), (256, 256), (64, 256), (256, 256), (64, 256), (256, 256),
        (64, 256), (8, 32), (4, 16), (9, 256, 256), (512, 256), (1024, 256),
    )
    flat = [a.reshape(s) for a, s in zip(args, shapes)]
    vm = pltpu.VMEM
    dma = pltpu.SemaphoreType.DMA
    outs = pl.pallas_call(
        kernel,
        out_shape=(
            jax.ShapeDtypeStruct((256, 512), BF16),
            jax.ShapeDtypeStruct((64, 1024), BF16),
            jax.ShapeDtypeStruct((72, 256), F32),
            jax.ShapeDtypeStruct((8,), F32),
            jax.ShapeDtypeStruct((16, 256), F32),
            jax.ShapeDtypeStruct((32, 256), F32),
        ),
        in_specs=[pl.BlockSpec(memory_space=pl.ANY)] * 13,
        out_specs=(
            pl.BlockSpec(memory_space=vm), pl.BlockSpec(memory_space=vm),
            pl.BlockSpec(memory_space=vm), pl.BlockSpec(memory_space=pltpu.SMEM),
            pl.BlockSpec(memory_space=vm), pl.BlockSpec(memory_space=vm),
        ),
        scratch_shapes=[vm(a.shape, a.dtype) for a in flat] + [
            vm((256, 256), BF16), vm((256, 64), BF16),
            vm((3, 320, 256), BF16), vm((3, 96, 256), BF16),
            vm((2, 48, 256), BF16), vm((2, 48, 256), BF16),
            vm((ROWS, 128), F32), vm((ROWS, 128), BF16), vm((ROWS, 128), BF16),
            vm((4, 4, 8, 16, 128), BF16), vm((4, 4, 8, 16, 128), BF16),
            vm((3, 4, 8, 16, 128), BF16), vm((3, 4, 8, 16, 128), BF16),
            vm((4, 8, 16, 128), BF16), vm((4, 8, 16, 128), BF16),
            vm((3, 8, 16, 128), BF16), vm((3, 8, 16, 128), BF16),
            vm((16, 16, 128), BF16), vm((16, 16, 128), BF16), vm((16, 16, 128), F32),
            dma((13,)), dma((2,)), dma((2,)), dma((5,)), dma((5,)), dma((6,)), dma((6,)),
            dma((6,)), dma((6,)), dma((16,)), dma((16,)), dma((16,)), dma((16,)),
            pltpu.SemaphoreType.REGULAR,
        ],
        compiler_params=pltpu.CompilerParams(
            collective_id=0, has_side_effects=True, vmem_limit_bytes=56 << 20
        ),
        name="pyramid_backward",
    )(*flat)
    t3, t4, head, bias, lat3, lat4 = outs
    return (t3.reshape(1, 8, 32, 512), t4.reshape(1, 4, 16, 1024), head, bias, lat3, lat4)


def solution(mesh):
    big = P("slide", "row", None, None)
    in_specs = (big,) * 8 + (P("slide", "row", None),) * 2 + (P(),) * 3
    out_specs = (big, big, P("row", None), P("row"), P("row", None), P("row", None))
    return jax.shard_map(local, mesh=mesh, in_specs=in_specs, out_specs=out_specs, check_vma=False)
```

```python
import jax
import jax.numpy as jnp
from jax import lax
from jax.experimental import pallas as pl
from jax.experimental.pallas import tpu as pltpu
from jax.sharding import PartitionSpec as P

MESH = pl.DeviceIdType.MESH
F32 = jnp.float32
BF16 = jnp.bfloat16
LOSS_SCALE = 256.0

ROW_BIAS = 2304
ROW_C3 = 2320
ROW_C4 = 2832
ROWS = 3856
CORE_PARTS = ((768, 768), (0, 768), (1536, 784), (ROW_C3, 512), (ROW_C4, 1024))
EARLY, LATE = (0, 5), (5, 3)
Z_ORDER = (8, 7, 9, 6, 10, 5, 11, 4, 12, 3, 13, 2, 14, 1, 15)
SLIDE_ORDER = (11, 10, 9, 8, 7, 15, 6, 14, 5, 13, 4, 12, 3, 2, 1)


def nt(a, b):
    return lax.dot_general(a, b, (((1,), (1,)), ((), ())), preferred_element_type=F32)


def nn(a, b):
    return jnp.dot(a, b, preferred_element_type=F32)


def kernel(
    tc3_h, tc4_h, f3_h, f4_h, p3_h, p4_h, g3_h, g4_h, k3_h, k4_h, hw_h, l3_h, l4_h,
    t3, t4, gath,
    piece,
    tc3, tc4, f3, f4, p3, p4, g3, g4, k3, k4, hw, l3, l4,
    f3t, f4t, c3t, c4t, edge_t, dx3, dx4, halo_s, halo_r, part, back_s, early, grads,
    core_s, core_r, bx, by, r1x, r1y, cx, cy, r2x, r2y, dz, r3,
    in_sem, halo_ss, halo_rs, core_ss, core_rs, s1_ss, s1_rs, s2_ss, s2_rs,
    z_ss, z_rs, ag_ss, ag_rs, far_sem,
):
    slide = lax.axis_index("slide")
    row = lax.axis_index("row")
    core = lax.rem(slide, 2)
    x_lo = lax.rem(slide // 2, 2)
    y = slide // 4
    z = row // 2
    x_hi = lax.rem(row, 2)
    x = 2 * x_hi + x_lo

    def dev(xx, yy, zz, cc):
        return ((yy * 2 + lax.rem(xx, 2)) * 2 + cc, zz * 2 + xx // 2)

    sibling = (slide + 1 - 2 * core, row)
    above = (slide, lax.rem(row + 31, 32))
    below = (slide, lax.rem(row + 1, 32))
    x_dev = [dev(lax.rem(x + d, 4), y, z, core) for d in (1, 2, 3)]
    y_dev = [dev(x, lax.rem(y + d, 4), z, core) for d in (1, 2, 3)]

    def z_dev(d):
        return dev(x, y, lax.rem(z + d + 16, 16), core)

    pairs = [
        (p3_h, p3), (g3_h, g3), (k3_h, k3), (k4_h, k4), (p4_h, p4), (g4_h, g4), (f3_h, f3),
        (f4_h, f4), (hw_h, hw), (tc3_h, tc3), (tc4_h, tc4), (l3_h, l3), (l4_h, l4),
    ]
    loads = [pltpu.make_async_copy(a, b, in_sem.at[i]) for i, (a, b) in enumerate(pairs)]
    barrier = pltpu.get_barrier_semaphore()
    partners = [above, below]
    partners += [z_dev(d) for d in (-4, 4, -3, 3, -2, 2, -1, 1)] + x_dev + y_dev + [sibling]
    for ld in loads[:6]:
        ld.start()
    for who in partners:
        pl.semaphore_signal(barrier, inc=1, device_id=who, device_id_type=MESH)

    for ld in loads[:6]:
        ld.wait()
    for ld in loads[6:]:
        ld.start()

    def delta(keep, pre, grad, height, width):
        keep_t = jnp.transpose(keep[...].astype(F32))
        cols = [jnp.broadcast_to(keep_t[:, i : i + 1], (width, 256)) for i in range(height)]
        mask = jnp.concatenate(cols, axis=0)
        live = jnp.logical_and(mask > 0.5, pre[...].astype(F32) > 0.0)
        return jnp.where(live, grad[...].astype(F32), 0.0)

    def put_shifted(dst, start, rows, width, val):
        col = lax.rem(lax.broadcasted_iota(jnp.int32, (rows, 256), 0), width)
        ahead = jnp.where(col == width - 1, 0.0, pltpu.roll(val, rows - 1, 0))
        behind = jnp.where(col == 0, 0.0, pltpu.roll(val, 1, 0))
        dst[0, start : start + rows, :] = ahead.astype(BF16)
        dst[1, start : start + rows, :] = val.astype(BF16)
        dst[2, start : start + rows, :] = behind.astype(BF16)

    d3 = delta(k3, p3, g3, 8, 32)
    d4 = delta(k4, p4, g4, 4, 16)
    halo_s[0, 0:32, :] = d3[0:32].astype(BF16)
    halo_s[0, 32:48, :] = d4[0:16].astype(BF16)
    halo_s[1, 0:32, :] = d3[224:256].astype(BF16)
    halo_s[1, 32:48, :] = d4[48:64].astype(BF16)

    pl.semaphore_wait(barrier, len(partners))
    halos = []
    for i, who in enumerate((above, below)):
        cp = pltpu.make_async_remote_copy(
            src_ref=halo_s.at[i], dst_ref=halo_r.at[i], send_sem=halo_ss.at[i],
            recv_sem=halo_rs.at[i], device_id=who, device_id_type=MESH,
        )
        cp.start()
        halos.append(cp)
    for d in (-4, 4):
        pl.semaphore_signal(far_sem, inc=1, device_id=z_dev(d), device_id_type=MESH)

    put_shifted(dx3, 32, 256, 32, d3)
    put_shifted(dx4, 16, 64, 16, d4)
    for b in range(3):
        dx3[b, 0:32, :] = jnp.zeros((32, 256), BF16)
        dx3[b, 288:320, :] = jnp.zeros((32, 256), BF16)
        dx4[b, 0:16, :] = jnp.zeros((16, 256), BF16)
        dx4[b, 80:96, :] = jnp.zeros((16, 256), BF16)

    first = core == 0

    def emit(start, rows, val):
        lo, hi = val[:, :128], val[:, 128:]
        grads[start : start + rows, :] = jnp.where(first, lo, hi)
        core_s[start : start + rows, :] = jnp.where(first, hi, lo).astype(BF16)

    core_copies = []

    def send_core(i):
        start, rows = CORE_PARTS[i]
        cp = pltpu.make_async_remote_copy(
            src_ref=core_s.at[pl.ds(start, rows)], dst_ref=core_r.at[pl.ds(start, rows)],
            send_sem=core_ss.at[i], recv_sem=core_rs.at[i], device_id=sibling,
            device_id_type=MESH,
        )
        cp.start()
        core_copies.append(cp)

    ones = jnp.ones((16, 256), BF16)
    bias = nn(ones, dx3[1, 32:288, :]) + nn(ones[:, :64], dx4[1, 16:80, :])
    emit(ROW_BIAS, 16, bias)
    loads[6].wait()
    loads[7].wait()
    f3t[...] = jnp.transpose(f3[...])
    f4t[...] = jnp.transpose(f4[...])
    edge_t[0] = jnp.transpose(jnp.concatenate([f3[0:32, :], f4[0:16, :]], axis=0))
    edge_t[1] = jnp.transpose(jnp.concatenate([f3[224:256, :], f4[48:64, :]], axis=0))

    def tap_term(a, b):
        top3, top4 = (2 - a) * 32, (2 - a) * 16
        val = nn(f3t[...], dx3[b, top3 : top3 + 256, :])
        return val + nn(f4t[...], dx4[b, top4 : top4 + 64, :])

    for b in range(3):
        emit((3 + b) * 256, 256, tap_term(1, b))
    send_core(0)
    loads[8].wait()
    back = jnp.zeros((320, 256), F32)
    for a in range(3):
        for b in range(3):
            top3, top4 = (2 - a) * 32, (2 - a) * 16
            patch = jnp.concatenate(
                [dx3[b, top3 : top3 + 256, :], dx4[b, top4 : top4 + 64, :]], axis=0
            )
            back = back + nt(patch, hw[3 * a + b])
    back_s[...] = back
    for b in range(3):
        part[b * 256 : b * 256 + 256, :] = tap_term(0, b)
        part[768 + b * 256 : 1024 + b * 256, :] = tap_term(2, b)
    loads[9].wait()
    loads[10].wait()
    c3t[...] = jnp.transpose(tc3[...])
    c4t[...] = jnp.transpose(tc4[...])
    inner = back_s[32:224, :].astype(BF16)
    early[...] = nn(c3t[:, 32:224], inner)
    loads[11].wait()
    loads[12].wait()
    t3[32:224, :] = nt(inner, l3[...]).astype(BF16)

    for cp in halos:
        cp.wait_recv()
    low = jnp.where(row < 31, halo_r[0].astype(F32), 0.0)
    top = jnp.where(row > 0, halo_r[1].astype(F32), 0.0)
    zero = jnp.zeros((48, 256), F32)

    def three(val):
        i = lax.broadcasted_iota(jnp.int32, (48, 256), 0)
        last = jnp.logical_or(i == 31, i == 47)
        start = jnp.logical_or(i == 0, i == 32)
        ahead = jnp.where(last, 0.0, pltpu.roll(val, 47, 0))
        behind = jnp.where(start, 0.0, pltpu.roll(val, 1, 0))
        return [v.astype(BF16) for v in (ahead, val, behind)]

    top3 = three(top)
    low3 = three(low)
    add_top = zero
    add_low = zero
    for b in range(3):
        add_top = add_top + nt(top3[b], hw[6 + b])
        add_low = add_low + nt(low3[b], hw[b])
    back_s[0:32, :] += add_top[0:32]
    back_s[224:256, :] += add_low[0:32]
    back_s[256:272, :] += add_top[32:48]
    back_s[304:320, :] += add_low[32:48]

    for b in range(3):
        emit(b * 256, 256, part[b * 256 : b * 256 + 256, :] + nn(edge_t[1], low3[b]))
    send_core(1)
    for b in range(3):
        emit(
            1536 + b * 256, 256,
            part[768 + b * 256 : 1024 + b * 256, :] + nn(edge_t[0], top3[b]),
        )
    send_core(2)

    back3 = back_s[0:256, :]
    lat3 = back3.astype(BF16)
    rest = (back3 - lat3.astype(F32)).astype(BF16)
    cell4 = lax.broadcasted_iota(jnp.int32, (64, 256), 0)
    cell3 = lax.broadcasted_iota(jnp.int32, (64, 256), 1)
    home = (cell3 // 64) * 16 + lax.rem(cell3, 32) // 2
    pool = jnp.where(home == cell4, 1.0, 0.0).astype(BF16)
    pooled = nn(pool, lat3) + nn(pool, rest)
    lat4 = (back_s[256:320, :] + pooled).astype(BF16)
    emit(
        ROW_C3, 512,
        early[...] + nn(c3t[:, 0:32], lat3[0:32]) + nn(c3t[:, 224:256], lat3[224:256]),
    )
    send_core(3)
    emit(ROW_C4, 1024, nn(c4t[...], lat4))
    send_core(4)


    def block(at):
        return grads[at : at + 16, :] + core_r[at : at + 16, :].astype(F32)

    def pack(half, kinds):
        for xx in range(4):
            xh, xl = xx // 2, xx % 2
            for yy in range(4):
                for kind in range(kinds[0], kinds[0] + kinds[1]):
                    pair = 8 * half + (kind - 2 * yy - xl) % 8
                    r = 2 * pair + xh
                    if kind < 4:
                        val = block(144 * pair + 80 * xh + 16 * kind)
                    elif kind == 4:
                        split = block(144 * pair + 64)
                        val = jnp.concatenate([split[8 * xh : 8 * xh + 8], bias_rows], axis=0)
                    elif kind == 5:
                        val = block(ROW_C3 + 16 * r)
                    else:
                        val = block(ROW_C4 + 32 * r + 16 * (kind - 6))
                    if half:
                        by[yy, kind, xx] = val.astype(BF16)
                    else:
                        bx[xx, kind, yy] = val.astype(BF16)

    def send_first(src, at, dst, who, kinds, base):
        out = []
        for d in (2, 1, 3):
            cp = pltpu.make_async_remote_copy(
                src_ref=src.at[lax.rem(at + d, 4), pl.ds(*kinds)],
                dst_ref=dst.at[d - 1, pl.ds(*kinds)],
                send_sem=s1_ss.at[base + d - 1], recv_sem=s1_rs.at[base + d - 1],
                device_id=who[d - 1], device_id_type=MESH,
            )
            cp.start()
            out.append(cp)
        return out

    def send_second(src, at, dst, who, kinds, base):
        out = []
        for d in (2, 1, 3):
            cp = pltpu.make_async_remote_copy(
                src_ref=src.at[lax.rem(at + d, 4), pl.ds(*kinds)],
                dst_ref=dst.at[d - 1, pl.ds(*kinds)],
                send_sem=s2_ss.at[base + d - 1], recv_sem=s2_rs.at[base + d - 1],
                device_id=who[d - 1], device_id_type=MESH,
            )
            cp.start()
            out.append(cp)
        return out

    def add_first(copies, src, at, got, out, kinds):
        for cp in copies:
            cp.wait_recv()
        for k in range(kinds[0], kinds[0] + kinds[1]):
            acc = src[at, k].astype(F32)
            for d in range(3):
                acc = acc + got[d, k].astype(F32)
            for i in range(4):
                out[i, k] = acc[i].astype(BF16)

    def add_second(copies, src, at, got, base, kinds):
        for cp in copies:
            cp.wait_recv()
        lo, n = kinds
        acc = src[at, lo : lo + n].astype(F32)
        for d in range(3):
            acc = acc + got[d, lo : lo + n].astype(F32)
        dz[base + lo : base + lo + n] = acc.astype(BF16)

    for cp in core_copies[:3]:
        cp.wait_recv()
    bias_rows = block(ROW_BIAS)[0:8]
    pack(0, EARLY)
    s1xa = send_first(bx, x, r1x, x_dev, EARLY, 0)
    pack(1, EARLY)
    s1ya = send_first(by, y, r1y, y_dev, EARLY, 3)

    t3[0:32, :] = nt(lat3[0:32], l3[...]).astype(BF16)
    t3[224:256, :] = nt(lat3[224:256], l3[...]).astype(BF16)
    t4[...] = nt(lat4, l4[...]).astype(BF16)

    for cp in core_copies[3:]:
        cp.wait_recv()
    pack(0, LATE)
    s1xb = send_first(bx, x, r1x, x_dev, LATE, 6)
    pack(1, LATE)
    s1yb = send_first(by, y, r1y, y_dev, LATE, 9)
    sends = list(halos) + list(core_copies) + s1xa + s1ya + s1xb + s1yb

    add_first(s1xa, bx, x, r1x, cx, EARLY)
    s2xa = send_second(cx, y, r2x, y_dev, EARLY, 0)
    add_first(s1ya, by, y, r1y, cy, EARLY)
    s2ya = send_second(cy, x, r2y, x_dev, EARLY, 3)
    add_first(s1xb, bx, x, r1x, cx, LATE)
    s2xb = send_second(cx, y, r2x, y_dev, LATE, 6)
    add_first(s1yb, by, y, r1y, cy, LATE)
    s2yb = send_second(cy, x, r2y, x_dev, LATE, 9)
    sends += s2xa + s2ya + s2xb + s2yb

    target = 2 * y + x_lo

    def slot(zz):
        return 8 * (zz // 8) + lax.rem(zz + target, 8)

    def z_copy(at, d):
        return pltpu.make_async_remote_copy(
            src_ref=dz.at[at], dst_ref=r3.at[d], send_sem=z_ss.at[d], recv_sem=z_rs.at[d],
            device_id=z_dev(d), device_id_type=MESH,
        )

    def send_z(early):
        for d in Z_ORDER:
            zz = lax.rem(z + d, 16)

            @pl.when((lax.rem(zz + target, 8) < 5) == early)
            def _():
                z_copy(slot(zz), d).start()

    add_second(s2xa, cx, y, r2x, 0, EARLY)
    add_second(s2ya, cy, x, r2y, 8, EARLY)
    pl.semaphore_wait(far_sem, 2)
    send_z(True)
    add_second(s2xb, cx, y, r2x, 0, LATE)
    add_second(s2yb, cy, x, r2y, 8, LATE)
    send_z(False)

    acc = dz[slot(z)].astype(F32)
    for d in reversed(Z_ORDER):
        z_copy(0, d).wait_recv()
        acc = acc + r3[d].astype(F32)

    piece[...] = (acc * (1.0 / LOSS_SCALE)).astype(BF16)
    home_slot = 2 * lax.rem(z + target, 8) + core
    gath[home_slot] = piece[...]
    gathers = []
    for o in SLIDE_ORDER:
        dy, dx, dc = o // 4, (o // 2) % 2, o % 2
        xl = lax.rem(x_lo + dx, 2)
        cc = lax.rem(core + dc, 2)
        cp = pltpu.make_async_remote_copy(
            src_ref=piece, dst_ref=gath.at[home_slot], send_sem=ag_ss.at[o],
            recv_sem=ag_rs.at[o], device_id=dev(2 * x_hi + xl, lax.rem(y + dy, 4), z, cc),
            device_id_type=MESH,
        )
        cp.start()
        gathers.append(cp)
    for cp in sends:
        cp.wait_send()
    for d in Z_ORDER:
        z_copy(0, d).wait_send()
    for cp in gathers:
        cp.wait()


def finish(t3, t4, gath, o_t3, o_t4, o_head, o_bias, o_l3, o_l4):
    row = lax.axis_index("row")
    o_t3[...] = t3[...]
    o_t4[...] = t4[...]
    odd = lax.rem(row, 2)
    halves = [gath[8 + c].astype(F32) for c in range(2)]
    for c in range(2):
        lanes = slice(128 * c, 128 * c + 128)

        @pl.when(odd == 0)
        def _():
            for blk in range(4):
                o_head[16 * blk : 16 * blk + 16, lanes] = gath[2 * blk + c].astype(F32)
            o_head[64:72, lanes] = halves[c][0:8]

        @pl.when(odd == 1)
        def _():
            o_head[0:8, lanes] = halves[c][0:8]
            for blk in range(4):
                o_head[8 + 16 * blk : 24 + 16 * blk, lanes] = gath[2 * blk + c].astype(F32)

        o_l3[:, lanes] = gath[10 + c].astype(F32)
        o_l4[0:16, lanes] = gath[12 + c].astype(F32)
        o_l4[16:32, lanes] = gath[14 + c].astype(F32)
    sums = jnp.concatenate([halves[0][8:16], halves[1][8:16]], axis=1)
    lane = lax.broadcasted_iota(jnp.int32, (8, 256), 1)
    sub = lax.broadcasted_iota(jnp.int32, (8, 256), 0)
    mine = jnp.where(lane == 8 * row + sub, sums, 0.0)
    for i in range(8):
        o_bias[i] = jnp.sum(mine[i : i + 1, :])


def local(*args):
    shapes = (
        (256, 512), (64, 1024), (256, 256), (64, 256), (256, 256), (64, 256), (256, 256),
        (64, 256), (8, 32), (4, 16), (9, 256, 256), (512, 256), (1024, 256),
    )
    flat = [a.reshape(s) for a, s in zip(args, shapes)]
    vm = pltpu.VMEM
    dma = pltpu.SemaphoreType.DMA
    in_vmem = pl.BlockSpec(memory_space=vm)
    anywhere = pl.BlockSpec(memory_space=pl.ANY)
    t3, t4, gath = pl.pallas_call(
        kernel,
        out_shape=(
            vm((256, 512), BF16), vm((64, 1024), BF16), vm((16, 16, 128), BF16),
        ),
        in_specs=[anywhere] * 13,
        out_specs=(in_vmem,) * 3,
        scratch_shapes=[
            vm((16, 128), BF16),
        ] + [vm(a.shape, a.dtype) for a in flat] + [
            vm((256, 256), BF16), vm((256, 64), BF16), vm((512, 256), BF16),
            vm((1024, 64), BF16), vm((2, 256, 48), BF16),
            vm((3, 320, 256), BF16), vm((3, 96, 256), BF16),
            vm((2, 48, 256), BF16), vm((2, 48, 256), BF16),
            vm((1536, 256), F32), vm((320, 256), F32), vm((512, 256), F32),
            vm((ROWS, 128), F32), vm((ROWS, 128), BF16), vm((ROWS, 128), BF16),
            vm((4, 8, 4, 16, 128), BF16), vm((4, 8, 4, 16, 128), BF16),
            vm((3, 8, 4, 16, 128), BF16), vm((3, 8, 4, 16, 128), BF16),
            vm((4, 8, 16, 128), BF16), vm((4, 8, 16, 128), BF16),
            vm((3, 8, 16, 128), BF16), vm((3, 8, 16, 128), BF16),
            vm((16, 16, 128), BF16), vm((16, 16, 128), BF16),
            dma((13,)), dma((2,)), dma((2,)), dma((5,)), dma((5,)), dma((12,)), dma((12,)),
            dma((12,)), dma((12,)), dma((16,)), dma((16,)), dma((16,)), dma((16,)),
            pltpu.SemaphoreType.REGULAR,
        ],
        compiler_params=pltpu.CompilerParams(
            collective_id=0, has_side_effects=True, vmem_limit_bytes=56 << 20
        ),
        name="pyramid_backward",
    )(*flat)
    outs = pl.pallas_call(
        finish,
        out_shape=(
            jax.ShapeDtypeStruct((256, 512), BF16),
            jax.ShapeDtypeStruct((64, 1024), BF16),
            jax.ShapeDtypeStruct((72, 256), F32),
            jax.ShapeDtypeStruct((8,), F32),
            jax.ShapeDtypeStruct((16, 256), F32),
            jax.ShapeDtypeStruct((32, 256), F32),
        ),
        in_specs=[in_vmem] * 3,
        out_specs=(
            in_vmem, in_vmem, in_vmem, pl.BlockSpec(memory_space=pltpu.SMEM), in_vmem, in_vmem,
        ),
        name="place_outputs",
    )(*[pltpu.with_memory_space_constraint(a, vm) for a in (t3, t4, gath)])
    t3, t4, head, bias, lat3, lat4 = outs
    return (t3.reshape(1, 8, 32, 512), t4.reshape(1, 4, 16, 1024), head, bias, lat3, lat4)


def solution(mesh):
    big = P("slide", "row", None, None)
    in_specs = (big,) * 8 + (P("slide", "row", None),) * 2 + (P(),) * 3
    out_specs = (big, big, P("row", None), P("row"), P("row", None), P("row", None))
    return jax.shard_map(local, mesh=mesh, in_specs=in_specs, out_specs=out_specs, check_vma=False)
```

```python
import jax
import jax.numpy as jnp
from jax import lax
from jax.experimental import pallas as pl
from jax.experimental.pallas import tpu as pltpu
from jax.sharding import PartitionSpec as P

MESH = pl.DeviceIdType.MESH
F32 = jnp.float32
BF16 = jnp.bfloat16
LOSS_SCALE = 256.0

ROW_BIAS = 2304
ROW_C3 = 2320
ROW_C4 = 2832
ROWS = 3856
ROWS_EARLY, ROWS_LATE = (0, ROW_BIAS), (ROW_BIAS, ROWS - ROW_BIAS)
EARLY, LATE = (0, 4), (4, 4)
P3, G3, P4, G4, F3, F4, HW, L3, L4, WIDE = 0, 256, 512, 576, 640, 896, 960, 3264, 3776, 4800
Z_ORDER = (8, 7, 9, 6, 10, 5, 11, 4, 12, 3, 13, 2, 14, 1, 15)
SLIDE_ORDER = (11, 10, 9, 8, 7, 15, 6, 14, 5, 13, 4, 12, 3, 2, 1)


def nt(a, b):
    return lax.dot_general(a, b, (((1,), (1,)), ((), ())), preferred_element_type=F32)


def nn(a, b):
    return jnp.dot(a, b, preferred_element_type=F32)


def kernel(
    tc3_h, tc4_h, f3_h, f4_h, p3_h, p4_h, g3_h, g4_h, k3_h, k4_h, hw_h, l3_h, l4_h,
    t3, t4, gath,
    piece, wide, tc3, tc4, k3, k4,
    f3t, f4t, c3t, c4t, edge_t, dx3, dx4, halo_s, halo_r, part, back_s, early, grads,
    core_s, core_r, bx, by, r1x, r1y, cx, cy, r2x, r2y, dz, r3,
    in_sem, halo_ss, halo_rs, core_ss, core_rs, s1_ss, s1_rs, s2_ss, s2_rs,
    z_ss, z_rs, ag_ss, ag_rs, far_sem,
):
    slide = lax.axis_index("slide")
    row = lax.axis_index("row")
    core = lax.rem(slide, 2)
    x_lo = lax.rem(slide // 2, 2)
    y = slide // 4
    z = row // 2
    x_hi = lax.rem(row, 2)
    x = 2 * x_hi + x_lo

    def dev(xx, yy, zz, cc):
        return ((yy * 2 + lax.rem(xx, 2)) * 2 + cc, zz * 2 + xx // 2)

    sibling = (slide + 1 - 2 * core, row)
    above = (slide, lax.rem(row + 31, 32))
    below = (slide, lax.rem(row + 1, 32))
    x_dev = [dev(lax.rem(x + d, 4), y, z, core) for d in (1, 2, 3)]
    y_dev = [dev(x, lax.rem(y + d, 4), z, core) for d in (1, 2, 3)]

    def z_dev(d):
        return dev(x, y, lax.rem(z + d + 16, 16), core)

    def load(src, dst, i):
        pltpu.make_async_copy(src, dst, in_sem.at[i]).start()

    def load_wide(src, at, rows, i):
        load(src, wide.at[pl.ds(at, rows)], i)

    def loaded(ref, i):
        pltpu.make_async_copy(ref, ref, in_sem.at[i]).wait()

    barrier = pltpu.get_barrier_semaphore()
    partners = [above, below]
    partners += [z_dev(d) for d in (-4, 4, -3, 3, -2, 2, -1, 1)] + x_dev + y_dev + [sibling]
    load_wide(p3_h, P3, 256, 0)
    load_wide(g3_h, G3, 256, 0)
    load_wide(p4_h, P4, 64, 0)
    load_wide(g4_h, G4, 64, 0)
    load(k3_h, k3, 1)
    load(k4_h, k4, 2)
    for who in partners:
        pl.semaphore_signal(barrier, inc=1, device_id=who, device_id_type=MESH)

    loaded(wide.at[pl.ds(0, 640)], 0)
    loaded(k3, 1)
    loaded(k4, 2)
    load_wide(f3_h, F3, 256, 3)
    load_wide(f4_h, F4, 64, 3)
    load_wide(hw_h, HW, 2304, 3)
    load_wide(l3_h, L3, 512, 3)
    load_wide(l4_h, L4, 1024, 3)
    load(tc3_h, tc3, 4)
    load(tc4_h, tc4, 5)

    def delta(keep, pre, grad, height, width):
        keep_t = jnp.transpose(keep[...].astype(F32))
        cols = [jnp.broadcast_to(keep_t[:, i : i + 1], (width, 256)) for i in range(height)]
        mask = jnp.concatenate(cols, axis=0)
        cells = height * width
        live = jnp.logical_and(mask > 0.5, wide[pre : pre + cells, :].astype(F32) > 0.0)
        return jnp.where(live, wide[grad : grad + cells, :].astype(F32), 0.0)

    def put_shifted(dst, start, rows, width, val):
        col = lax.rem(lax.broadcasted_iota(jnp.int32, (rows, 256), 0), width)
        ahead = jnp.where(col == width - 1, 0.0, pltpu.roll(val, rows - 1, 0))
        behind = jnp.where(col == 0, 0.0, pltpu.roll(val, 1, 0))
        dst[0, start : start + rows, :] = ahead.astype(BF16)
        dst[1, start : start + rows, :] = val.astype(BF16)
        dst[2, start : start + rows, :] = behind.astype(BF16)

    d3 = delta(k3, P3, G3, 8, 32)
    d4 = delta(k4, P4, G4, 4, 16)
    halo_s[0, 0:32, :] = d3[0:32].astype(BF16)
    halo_s[0, 32:48, :] = d4[0:16].astype(BF16)
    halo_s[1, 0:32, :] = d3[224:256].astype(BF16)
    halo_s[1, 32:48, :] = d4[48:64].astype(BF16)

    pl.semaphore_wait(barrier, len(partners))
    for i, who in enumerate((above, below)):
        pltpu.make_async_remote_copy(
            src_ref=halo_s.at[i], dst_ref=halo_r.at[i], send_sem=halo_ss.at[0],
            recv_sem=halo_rs.at[i], device_id=who, device_id_type=MESH,
        ).start()
    for d in (-4, 4):
        pl.semaphore_signal(far_sem, inc=1, device_id=z_dev(d), device_id_type=MESH)

    put_shifted(dx3, 32, 256, 32, d3)
    put_shifted(dx4, 16, 64, 16, d4)
    for b in range(3):
        dx3[b, 0:32, :] = jnp.zeros((32, 256), BF16)
        dx3[b, 288:320, :] = jnp.zeros((32, 256), BF16)
        dx4[b, 0:16, :] = jnp.zeros((16, 256), BF16)
        dx4[b, 80:96, :] = jnp.zeros((16, 256), BF16)

    first = core == 0

    def emit(start, rows, val):
        lo, hi = val[:, :128], val[:, 128:]
        at = pl.ds(start, rows)
        grads[at, :] = jnp.where(first, lo, hi)
        core_s[at, :] = jnp.where(first, hi, lo).astype(BF16)

    def core_copy(start, rows, i):
        at = pl.ds(start, rows)
        return pltpu.make_async_remote_copy(
            src_ref=core_s.at[at], dst_ref=core_r.at[at], send_sem=core_ss.at[0],
            recv_sem=core_rs.at[i], device_id=sibling, device_id_type=MESH,
        )

    ones = jnp.ones((16, 256), BF16)
    bias = nn(ones, dx3[1, 32:288, :]) + nn(ones[:, :64], dx4[1, 16:80, :])
    emit(ROW_BIAS, 16, bias)
    loaded(wide.at[pl.ds(F3, WIDE - F3)], 3)
    f3t[...] = jnp.transpose(wide[F3 : F3 + 256, :])
    f4t[...] = jnp.transpose(wide[F4 : F4 + 64, :])
    for i, (at3, at4) in enumerate(((F3, F4), (F3 + 224, F4 + 48))):
        edge = jnp.concatenate([wide[at3 : at3 + 32, :], wide[at4 : at4 + 16, :]], axis=0)
        edge_t[i] = jnp.transpose(edge)

    def tap_term(a, b):
        top3, top4 = (2 - a) * 32, (2 - a) * 16
        val = nn(f3t[...], dx3[b, top3 : top3 + 256, :])
        return val + nn(f4t[...], dx4[b, top4 : top4 + 64, :])

    for b in range(3):
        emit((3 + b) * 256, 256, tap_term(1, b))
    core_copy(768, 768, 0).start()
    back = jnp.zeros((320, 256), F32)
    for a in range(3):
        for b in range(3):
            top3, top4 = (2 - a) * 32, (2 - a) * 16
            patch = jnp.concatenate(
                [dx3[b, top3 : top3 + 256, :], dx4[b, top4 : top4 + 64, :]], axis=0
            )
            at = HW + 256 * (3 * a + b)
            back = back + nt(patch, wide[at : at + 256, :])
    back_s[...] = back
    for b in range(3):
        part[b * 256 : b * 256 + 256, :] = tap_term(0, b)
        part[768 + b * 256 : 1024 + b * 256, :] = tap_term(2, b)
    loaded(tc3, 4)
    loaded(tc4, 5)
    c3t[...] = jnp.transpose(tc3[...])
    c4t[...] = jnp.transpose(tc4[...])
    inner = back_s[32:224, :].astype(BF16)
    early[...] = nn(c3t[:, 32:224], inner)
    l3, l4 = wide[L3 : L3 + 512, :], wide[L4 : L4 + 1024, :]
    t3[32:224, :] = nt(inner, l3).astype(BF16)

    def three(val):
        i = lax.broadcasted_iota(jnp.int32, (48, 256), 0)
        last = jnp.logical_or(i == 31, i == 47)
        start = jnp.logical_or(i == 0, i == 32)
        ahead = jnp.where(last, 0.0, pltpu.roll(val, 47, 0))
        behind = jnp.where(start, 0.0, pltpu.roll(val, 1, 0))
        return [v.astype(BF16) for v in (ahead, val, behind)]

    def edge_side(side):
        pltpu.make_async_remote_copy(
            src_ref=halo_s.at[side], dst_ref=halo_r.at[side], send_sem=halo_ss.at[0],
            recv_sem=halo_rs.at[side], device_id=above, device_id_type=MESH,
        ).wait_recv()
        valid = jnp.where(side == 0, row, 31 - row) < 31
        shifted = three(jnp.where(valid, halo_r[side].astype(F32), 0.0))
        start = pl.multiple_of(side * 1536, 256)
        half = pl.multiple_of(side * 768, 256)
        for b in range(3):
            val = part[pl.ds(half + b * 256, 256), :] + nn(edge_t[1 - side], shifted[b])
            emit(start + b * 256, 256, val)
        core_copy(start, 768, 0).start()
        add = jnp.zeros((48, 256), F32)
        for b in range(3):
            at = pl.multiple_of(HW + 1536 * side + 256 * b, 64)
            add = add + nt(shifted[b], wide[pl.ds(at, 256), :])
        at3 = pl.ds(pl.multiple_of(224 * (1 - side), 32), 32)
        at4 = pl.ds(pl.multiple_of(256 + 48 * (1 - side), 16), 16)
        back_s[at3, :] += add[0:32]
        back_s[at4, :] += add[32:48]

    edge_side(x_hi)
    edge_side(1 - x_hi)

    back3 = back_s[0:256, :]
    lat3 = back3.astype(BF16)
    rest = (back3 - lat3.astype(F32)).astype(BF16)
    cell4 = lax.broadcasted_iota(jnp.int32, (64, 256), 0)
    cell3 = lax.broadcasted_iota(jnp.int32, (64, 256), 1)
    home = (cell3 // 64) * 16 + lax.rem(cell3, 32) // 2
    pool = jnp.where(home == cell4, 1.0, 0.0).astype(BF16)
    pooled = nn(pool, lat3) + nn(pool, rest)
    lat4 = (back_s[256:320, :] + pooled).astype(BF16)
    emit(
        ROW_C3, 512,
        early[...] + nn(c3t[:, 0:32], lat3[0:32]) + nn(c3t[:, 224:256], lat3[224:256]),
    )
    core_copy(ROW_BIAS, 528, 1).start()
    emit(ROW_C4, 1024, nn(c4t[...], lat4))
    core_copy(ROW_C4, 1024, 1).start()


    def block(at):
        return grads[at : at + 16, :] + core_r[at : at + 16, :].astype(F32)

    def pack(half, kinds, bias_rows=None):
        for xx in range(4):
            xh, xl = xx // 2, xx % 2
            for yy in range(4):
                for kind in range(kinds[0], kinds[0] + kinds[1]):
                    pair = 8 * half + (kind - 2 * yy - xl) % 8
                    r = 2 * pair + xh
                    if kind < 4:
                        val = block(144 * pair + 80 * xh + 16 * kind)
                    elif kind == 4:
                        split = block(144 * pair + 64)
                        val = jnp.concatenate([split[8 * xh : 8 * xh + 8], bias_rows], axis=0)
                    elif kind == 5:
                        val = block(ROW_C3 + 16 * r)
                    else:
                        val = block(ROW_C4 + 32 * r + 16 * (kind - 6))
                    if half:
                        by[yy, kind, xx] = val.astype(BF16)
                    else:
                        bx[xx, kind, yy] = val.astype(BF16)

    def first_copy(src, at, dst, who, kinds, axis, late):
        blocks = pl.ds(*kinds)
        return pltpu.make_async_remote_copy(
            src_ref=src.at[at, blocks], dst_ref=dst.at[who, blocks], send_sem=s1_ss.at[axis],
            recv_sem=s1_rs.at[2 * axis + late],
            device_id=(x_dev, y_dev)[axis][who], device_id_type=MESH,
        )

    def send_first(src, at, dst, kinds, axis, late):
        for d in (2, 1, 3):
            first_copy(src, lax.rem(at + d, 4), dst, d - 1, kinds, axis, late).start()

    def second_copy(src, at, dst, who, kinds, axis, late):
        blocks = pl.ds(*kinds)
        return pltpu.make_async_remote_copy(
            src_ref=src.at[at, blocks], dst_ref=dst.at[who, blocks], send_sem=s2_ss.at[axis],
            recv_sem=s2_rs.at[2 * axis + late],
            device_id=(x_dev, y_dev)[axis][who], device_id_type=MESH,
        )

    def send_second(src, at, dst, kinds, axis, late):
        for d in (2, 1, 3):
            second_copy(src, lax.rem(at + d, 4), dst, d - 1, kinds, axis, late).start()

    def arrived(ref, sem):
        pltpu.make_async_copy(ref, ref, sem).wait()

    def add_first(src, at, got, out, kinds, axis, late):
        arrived(got.at[:, pl.ds(*kinds)], s1_rs.at[2 * axis + late])
        for k in range(kinds[0], kinds[0] + kinds[1]):
            acc = src[at, k].astype(F32)
            for d in range(3):
                acc = acc + got[d, k].astype(F32)
            for i in range(4):
                out[i, k] = acc[i].astype(BF16)

    def add_second(src, at, got, base, kinds, axis, late):
        arrived(got.at[:, pl.ds(*kinds)], s2_rs.at[2 * axis + late])
        lo, n = kinds
        acc = src[at, lo : lo + n].astype(F32)
        for d in range(3):
            acc = acc + got[d, lo : lo + n].astype(F32)
        dz[base + lo : base + lo + n] = acc.astype(BF16)

    arrived(core_r.at[pl.ds(*ROWS_EARLY)], core_rs.at[0])
    pack(0, EARLY)
    send_first(bx, x, r1x, EARLY, 0, 0)
    pack(1, EARLY)
    send_first(by, y, r1y, EARLY, 1, 0)

    t3[0:32, :] = nt(lat3[0:32], l3).astype(BF16)
    t3[224:256, :] = nt(lat3[224:256], l3).astype(BF16)
    t4[...] = nt(lat4, l4).astype(BF16)

    arrived(core_r.at[pl.ds(*ROWS_LATE)], core_rs.at[1])
    bias_rows = block(ROW_BIAS)[0:8]
    pack(0, LATE, bias_rows)
    send_first(bx, x, r1x, LATE, 0, 1)
    pack(1, LATE, bias_rows)
    send_first(by, y, r1y, LATE, 1, 1)

    add_first(bx, x, r1x, cx, EARLY, 0, 0)
    send_second(cx, y, r2x, EARLY, 1, 0)
    add_first(by, y, r1y, cy, EARLY, 1, 0)
    send_second(cy, x, r2y, EARLY, 0, 0)
    add_first(bx, x, r1x, cx, LATE, 0, 1)
    send_second(cx, y, r2x, LATE, 1, 1)
    add_first(by, y, r1y, cy, LATE, 1, 1)
    send_second(cy, x, r2y, LATE, 0, 1)

    target = 2 * y + x_lo

    def slot(zz):
        return 8 * (zz // 8) + lax.rem(zz + target, 8)

    def z_copy(at, d):
        return pltpu.make_async_remote_copy(
            src_ref=dz.at[at], dst_ref=r3.at[d], send_sem=z_ss.at[0], recv_sem=z_rs.at[0],
            device_id=z_dev(d), device_id_type=MESH,
        )

    def send_z(early):
        for d in Z_ORDER:
            zz = lax.rem(z + d, 16)

            @pl.when((lax.rem(zz + target, 8) < 4) == early)
            def _():
                z_copy(slot(zz), d).start()

    add_second(cx, y, r2x, 0, EARLY, 1, 0)
    add_second(cy, x, r2y, 8, EARLY, 0, 0)
    pl.semaphore_wait(far_sem, 2)
    send_z(True)
    add_second(cx, y, r2x, 0, LATE, 1, 1)
    add_second(cy, x, r2y, 8, LATE, 0, 1)
    send_z(False)

    arrived(r3.at[pl.ds(1, 15)], z_rs.at[0])
    acc = dz[slot(z)].astype(F32)
    for d in range(1, 16):
        acc = acc + r3[d].astype(F32)

    piece[...] = (acc * (1.0 / LOSS_SCALE)).astype(BF16)
    home_slot = 2 * lax.rem(z + target, 8) + core
    gath[home_slot] = piece[...]
    for o in SLIDE_ORDER:
        dy, dx, dc = o // 4, (o // 2) % 2, o % 2
        xl = lax.rem(x_lo + dx, 2)
        cc = lax.rem(core + dc, 2)
        pltpu.make_async_remote_copy(
            src_ref=piece, dst_ref=gath.at[home_slot], send_sem=ag_ss.at[0],
            recv_sem=ag_rs.at[0], device_id=dev(2 * x_hi + xl, lax.rem(y + dy, 4), z, cc),
            device_id_type=MESH,
        ).start()

    arrived(halo_s, halo_ss.at[0])
    arrived(core_s, core_ss.at[0])
    for axis in range(2):
        arrived(bx.at[pl.ds(0, 3)], s1_ss.at[axis])
        arrived(cx.at[pl.ds(0, 3)], s2_ss.at[axis])
    arrived(dz.at[pl.ds(0, 15)], z_ss.at[0])
    arrived(gath.at[pl.ds(0, 15)], ag_ss.at[0])
    arrived(gath.at[pl.ds(0, 15)], ag_rs.at[0])


def finish(t3, t4, gath, o_t3, o_t4, o_head, o_bias, o_l3, o_l4):
    row = lax.axis_index("row")
    o_t3[...] = t3[...]
    o_t4[...] = t4[...]
    odd = lax.rem(row, 2)
    halves = [gath[8 + c].astype(F32) for c in range(2)]
    for c in range(2):
        lanes = slice(128 * c, 128 * c + 128)

        @pl.when(odd == 0)
        def _():
            for blk in range(4):
                o_head[16 * blk : 16 * blk + 16, lanes] = gath[2 * blk + c].astype(F32)
            o_head[64:72, lanes] = halves[c][0:8]

        @pl.when(odd == 1)
        def _():
            o_head[0:8, lanes] = halves[c][0:8]
            for blk in range(4):
                o_head[8 + 16 * blk : 24 + 16 * blk, lanes] = gath[2 * blk + c].astype(F32)

        o_l3[:, lanes] = gath[10 + c].astype(F32)
        o_l4[0:16, lanes] = gath[12 + c].astype(F32)
        o_l4[16:32, lanes] = gath[14 + c].astype(F32)
    sums = jnp.concatenate([halves[0][8:16], halves[1][8:16]], axis=1)
    lane = lax.broadcasted_iota(jnp.int32, (8, 256), 1)
    sub = lax.broadcasted_iota(jnp.int32, (8, 256), 0)
    mine = jnp.where(lane == 8 * row + sub, sums, 0.0)
    for i in range(8):
        o_bias[i] = jnp.sum(mine[i : i + 1, :])


def local(*args):
    shapes = (
        (256, 512), (64, 1024), (256, 256), (64, 256), (256, 256), (64, 256), (256, 256),
        (64, 256), (8, 32), (4, 16), (2304, 256), (512, 256), (1024, 256),
    )
    flat = [a.reshape(s) for a, s in zip(args, shapes)]
    vm = pltpu.VMEM
    dma = pltpu.SemaphoreType.DMA
    in_vmem = pl.BlockSpec(memory_space=vm)
    anywhere = pl.BlockSpec(memory_space=pl.ANY)
    t3, t4, gath = pl.pallas_call(
        kernel,
        out_shape=(
            vm((256, 512), BF16), vm((64, 1024), BF16), vm((16, 16, 128), BF16),
        ),
        in_specs=[anywhere] * 13,
        out_specs=(in_vmem,) * 3,
        scratch_shapes=[
            vm((16, 128), BF16), vm((WIDE, 256), BF16), vm((256, 512), BF16),
            vm((64, 1024), BF16), vm((8, 32), jnp.int32), vm((4, 16), jnp.int32),
            vm((256, 256), BF16), vm((256, 64), BF16), vm((512, 256), BF16),
            vm((1024, 64), BF16), vm((2, 256, 48), BF16),
            vm((3, 320, 256), BF16), vm((3, 96, 256), BF16),
            vm((2, 48, 256), BF16), vm((2, 48, 256), BF16),
            vm((1536, 256), F32), vm((320, 256), F32), vm((512, 256), F32),
            vm((ROWS, 128), F32), vm((ROWS, 128), BF16), vm((ROWS, 128), BF16),
            vm((4, 8, 4, 16, 128), BF16), vm((4, 8, 4, 16, 128), BF16),
            vm((3, 8, 4, 16, 128), BF16), vm((3, 8, 4, 16, 128), BF16),
            vm((4, 8, 16, 128), BF16), vm((4, 8, 16, 128), BF16),
            vm((3, 8, 16, 128), BF16), vm((3, 8, 16, 128), BF16),
            vm((16, 16, 128), BF16), vm((16, 16, 128), BF16),
            dma((6,)), dma((1,)), dma((2,)), dma((1,)), dma((2,)), dma((2,)), dma((4,)),
            dma((2,)), dma((4,)), dma((1,)), dma((1,)), dma((1,)), dma((1,)),
            pltpu.SemaphoreType.REGULAR,
        ],
        compiler_params=pltpu.CompilerParams(
            collective_id=0, has_side_effects=True, vmem_limit_bytes=56 << 20
        ),
        name="pyramid_backward",
    )(*flat)
    outs = pl.pallas_call(
        finish,
        out_shape=(
            jax.ShapeDtypeStruct((256, 512), BF16),
            jax.ShapeDtypeStruct((64, 1024), BF16),
            jax.ShapeDtypeStruct((72, 256), F32),
            jax.ShapeDtypeStruct((8,), F32),
            jax.ShapeDtypeStruct((16, 256), F32),
            jax.ShapeDtypeStruct((32, 256), F32),
        ),
        in_specs=[in_vmem] * 3,
        out_specs=(
            in_vmem, in_vmem, in_vmem, pl.BlockSpec(memory_space=pltpu.SMEM), in_vmem, in_vmem,
        ),
        name="place_outputs",
    )(*[pltpu.with_memory_space_constraint(a, vm) for a in (t3, t4, gath)])
    t3, t4, head, bias, lat3, lat4 = outs
    return (t3.reshape(1, 8, 32, 512), t4.reshape(1, 4, 16, 1024), head, bias, lat3, lat4)


def solution(mesh):
    big = P("slide", "row", None, None)
    in_specs = (big,) * 8 + (P("slide", "row", None),) * 2 + (P(),) * 3
    out_specs = (big, big, P("row", None), P("row"), P("row", None), P("row", None))
    return jax.shard_map(local, mesh=mesh, in_specs=in_specs, out_specs=out_specs, check_vma=False)
```

```python
import jax
import jax.numpy as jnp
from jax import lax
from jax.experimental import pallas as pl
from jax.experimental.pallas import tpu as pltpu
from jax.sharding import PartitionSpec as P

MESH = pl.DeviceIdType.MESH
F32 = jnp.float32
BF16 = jnp.bfloat16
LOSS_SCALE = 256.0

ROW_BIAS = 2304
ROW_C3 = 2320
ROW_C4 = 2832
ROWS = 3856
AHEAD, NEXT, REST = (0, 2), (2, 2), (4, 4)
C3_AHEAD, C4_AHEAD = 128, 256
ROWS_AHEAD = 768 + 16 + C3_AHEAD + C4_AHEAD
P3, G3, P4, G4, F3, F4, HW, L3, L4, WIDE = 0, 256, 512, 576, 640, 896, 960, 3264, 3776, 4800
PLANES_REST = (15, 14, 13, 12, 11, 10, 9, 8)
SLIDE_ORDER = (11, 10, 9, 8, 7, 15, 6, 14, 5, 13, 4, 12, 3, 2, 1)


def nt(a, b):
    return lax.dot_general(a, b, (((1,), (1,)), ((), ())), preferred_element_type=F32)


def nn(a, b):
    return jnp.dot(a, b, preferred_element_type=F32)


def kernel(
    tc3_h, tc4_h, f3_h, f4_h, p3_h, p4_h, g3_h, g4_h, k3_h, k4_h, hw_h, l3_h, l4_h,
    t3, t4, gath,
    piece, wide, tc3, tc4, k3, k4,
    f3t, f4t, c3t, c4t, edge_t, dx3, dx4, halo_s, halo_r, part, back_s, early, grads,
    core_s, core_r, bx, by, r1x, r1y, cx, cy, r2x, r2y, dz, r3,
    in_sem, halo_ss, halo_rs, core_ss, core_rs, s1_ss, s1_rs, s2_ss, s2_rs,
    z_ss, z_rs, ag_ss, ag_rs, far_sem,
):
    slide = lax.axis_index("slide")
    row = lax.axis_index("row")
    core = lax.rem(slide, 2)
    x_lo = lax.rem(slide // 2, 2)
    y = slide // 4
    z = row // 2
    x_hi = lax.rem(row, 2)
    x = 2 * x_hi + x_lo

    def dev(xx, yy, zz, cc):
        return ((yy * 2 + lax.rem(xx, 2)) * 2 + cc, zz * 2 + xx // 2)

    sibling = (slide + 1 - 2 * core, row)
    above = (slide, lax.rem(row + 31, 32))
    below = (slide, lax.rem(row + 1, 32))
    x_dev = [dev(lax.rem(x + d, 4), y, z, core) for d in (1, 2, 3)]
    y_dev = [dev(x, lax.rem(y + d, 4), z, core) for d in (1, 2, 3)]

    def z_dev(d):
        return dev(x, y, lax.rem(z + d + 16, 16), core)

    def load(src, dst, i):
        pltpu.make_async_copy(src, dst, in_sem.at[i]).start()

    def load_wide(src, at, rows, i):
        load(src, wide.at[pl.ds(at, rows)], i)

    def loaded(ref, i):
        pltpu.make_async_copy(ref, ref, in_sem.at[i]).wait()

    barrier = pltpu.get_barrier_semaphore()
    partners = [above, below]
    partners += [z_dev(d) for d in (-4, 4, -3, 3, -2, 2, -1, 1)] + x_dev + y_dev + [sibling]
    load_wide(p3_h, P3, 256, 0)
    load_wide(g3_h, G3, 256, 0)
    load_wide(p4_h, P4, 64, 0)
    load_wide(g4_h, G4, 64, 0)
    load(k3_h, k3, 1)
    load(k4_h, k4, 2)
    for who in partners:
        pl.semaphore_signal(barrier, inc=1, device_id=who, device_id_type=MESH)

    loaded(wide.at[pl.ds(0, 640)], 0)
    loaded(k3, 1)
    loaded(k4, 2)
    load_wide(f3_h, F3, 256, 3)
    load_wide(f4_h, F4, 64, 3)
    load_wide(hw_h, HW, 2304, 3)
    load_wide(l3_h, L3, 512, 3)
    load_wide(l4_h, L4, 1024, 3)
    load(tc3_h, tc3, 4)
    load(tc4_h, tc4, 5)

    def delta(keep, pre, grad, height, width):
        keep_t = jnp.transpose(keep[...].astype(F32))
        cols = [jnp.broadcast_to(keep_t[:, i : i + 1], (width, 256)) for i in range(height)]
        mask = jnp.concatenate(cols, axis=0)
        cells = height * width
        live = jnp.logical_and(mask > 0.5, wide[pre : pre + cells, :].astype(F32) > 0.0)
        return jnp.where(live, wide[grad : grad + cells, :].astype(F32), 0.0)

    def put_shifted(dst, start, rows, width, val):
        col = lax.rem(lax.broadcasted_iota(jnp.int32, (rows, 256), 0), width)
        ahead = jnp.where(col == width - 1, 0.0, pltpu.roll(val, rows - 1, 0))
        behind = jnp.where(col == 0, 0.0, pltpu.roll(val, 1, 0))
        dst[0, start : start + rows, :] = ahead.astype(BF16)
        dst[1, start : start + rows, :] = val.astype(BF16)
        dst[2, start : start + rows, :] = behind.astype(BF16)

    d3 = delta(k3, P3, G3, 8, 32)
    d4 = delta(k4, P4, G4, 4, 16)
    halo_s[0, 0:32, :] = d3[0:32].astype(BF16)
    halo_s[0, 32:48, :] = d4[0:16].astype(BF16)
    halo_s[1, 0:32, :] = d3[224:256].astype(BF16)
    halo_s[1, 32:48, :] = d4[48:64].astype(BF16)

    pl.semaphore_wait(barrier, len(partners))
    for i, who in enumerate((above, below)):
        pltpu.make_async_remote_copy(
            src_ref=halo_s.at[i], dst_ref=halo_r.at[i], send_sem=halo_ss.at[0],
            recv_sem=halo_rs.at[i], device_id=who, device_id_type=MESH,
        ).start()
    for d in (-4, 4):
        pl.semaphore_signal(far_sem, inc=1, device_id=z_dev(d), device_id_type=MESH)

    put_shifted(dx3, 32, 256, 32, d3)
    put_shifted(dx4, 16, 64, 16, d4)
    for b in range(3):
        dx3[b, 0:32, :] = jnp.zeros((32, 256), BF16)
        dx3[b, 288:320, :] = jnp.zeros((32, 256), BF16)
        dx4[b, 0:16, :] = jnp.zeros((16, 256), BF16)
        dx4[b, 80:96, :] = jnp.zeros((16, 256), BF16)

    first = core == 0

    def emit(start, rows, val):
        lo, hi = val[:, :128], val[:, 128:]
        at = pl.ds(start, rows)
        grads[at, :] = jnp.where(first, lo, hi)
        core_s[at, :] = jnp.where(first, hi, lo).astype(BF16)

    def core_copy(start, rows, i):
        at = pl.ds(start, rows)
        return pltpu.make_async_remote_copy(
            src_ref=core_s.at[at], dst_ref=core_r.at[at], send_sem=core_ss.at[0],
            recv_sem=core_rs.at[i], device_id=sibling, device_id_type=MESH,
        )

    ones = jnp.ones((16, 256), BF16)
    bias = nn(ones, dx3[1, 32:288, :]) + nn(ones[:, :64], dx4[1, 16:80, :])
    emit(ROW_BIAS, 16, bias)
    loaded(wide.at[pl.ds(F3, WIDE - F3)], 3)
    f3t[...] = jnp.transpose(wide[F3 : F3 + 256, :])
    f4t[...] = jnp.transpose(wide[F4 : F4 + 64, :])
    for i, (at3, at4) in enumerate(((F3, F4), (F3 + 224, F4 + 48))):
        edge = jnp.concatenate([wide[at3 : at3 + 32, :], wide[at4 : at4 + 16, :]], axis=0)
        edge_t[i] = jnp.transpose(edge)

    def tap_term(a, b):
        top3, top4 = (2 - a) * 32, (2 - a) * 16
        val = nn(f3t[...], dx3[b, top3 : top3 + 256, :])
        return val + nn(f4t[...], dx4[b, top4 : top4 + 64, :])

    for b in range(3):
        emit((3 + b) * 256, 256, tap_term(1, b))
    core_copy(768, 768, 1).start()
    back = jnp.zeros((320, 256), F32)
    for a in range(3):
        for b in range(3):
            top3, top4 = (2 - a) * 32, (2 - a) * 16
            patch = jnp.concatenate(
                [dx3[b, top3 : top3 + 256, :], dx4[b, top4 : top4 + 64, :]], axis=0
            )
            at = HW + 256 * (3 * a + b)
            back = back + nt(patch, wide[at : at + 256, :])
    back_s[...] = back
    for b in range(3):
        part[b * 256 : b * 256 + 256, :] = tap_term(0, b)
        part[768 + b * 256 : 1024 + b * 256, :] = tap_term(2, b)
    loaded(tc3, 4)
    loaded(tc4, 5)
    c3t[...] = jnp.transpose(tc3[...])
    c4t[...] = jnp.transpose(tc4[...])
    inner = back_s[32:224, :].astype(BF16)
    early[...] = nn(c3t[:, 32:224], inner)
    l3, l4 = wide[L3 : L3 + 512, :], wide[L4 : L4 + 1024, :]
    t3[32:224, :] = nt(inner, l3).astype(BF16)

    def edge_side(side):
        pltpu.make_async_remote_copy(
            src_ref=halo_s.at[side], dst_ref=halo_r.at[side], send_sem=halo_ss.at[0],
            recv_sem=halo_rs.at[side], device_id=above, device_id_type=MESH,
        ).wait_recv()
        valid = row > 0 if side else row < 31
        val = jnp.where(valid, halo_r[side].astype(F32), 0.0)
        i = lax.broadcasted_iota(jnp.int32, (48, 256), 0)
        last = jnp.logical_or(i == 31, i == 47)
        start = jnp.logical_or(i == 0, i == 32)
        ahead = jnp.where(last, 0.0, pltpu.roll(val, 47, 0))
        behind = jnp.where(start, 0.0, pltpu.roll(val, 1, 0))
        return [v.astype(BF16) for v in (ahead, val, behind)]

    def edge_back(side, shifted):
        add = jnp.zeros((48, 256), F32)
        for b in range(3):
            at = HW + 1536 * side + 256 * b
            add = add + nt(shifted[b], wide[at : at + 256, :])
        at3, at4 = 224 * (1 - side), 256 + 48 * (1 - side)
        back_s[at3 : at3 + 32, :] += add[0:32]
        back_s[at4 : at4 + 16, :] += add[32:48]

    def edge_head(side, shifted):
        for b in range(3):
            at = 768 * side + 256 * b
            val = part[at : at + 256, :] + nn(edge_t[1 - side], shifted[b])
            emit(1536 * side + 256 * b, 256, val)

    low = edge_side(0)
    edge_head(0, low)
    core_copy(0, 768, 0).start()
    edge_back(0, low)
    top = edge_side(1)
    edge_back(1, top)

    back3 = back_s[0:256, :]
    lat3 = back3.astype(BF16)
    rest = (back3 - lat3.astype(F32)).astype(BF16)
    cell4 = lax.broadcasted_iota(jnp.int32, (64, 256), 0)
    cell3 = lax.broadcasted_iota(jnp.int32, (64, 256), 1)
    home = (cell3 // 64) * 16 + lax.rem(cell3, 32) // 2
    pool = jnp.where(home == cell4, 1.0, 0.0).astype(BF16)
    pooled = nn(pool, lat3) + nn(pool, rest)
    lat4 = (back_s[256:320, :] + pooled).astype(BF16)

    def emit_c3(lo, hi):
        val = early[lo:hi, :] + nn(c3t[lo:hi, 0:32], lat3[0:32])
        val = val + nn(c3t[lo:hi, 224:256], lat3[224:256])
        emit(ROW_C3 + lo, hi - lo, val)

    def emit_c4(lo, hi):
        emit(ROW_C4 + lo, hi - lo, nn(c4t[lo:hi, :], lat4))

    emit_c3(0, C3_AHEAD)
    core_copy(ROW_BIAS, 16 + C3_AHEAD, 0).start()
    emit_c4(0, C4_AHEAD)
    core_copy(ROW_C4, C4_AHEAD, 0).start()
    edge_head(1, top)
    core_copy(1536, 768, 1).start()
    emit_c3(C3_AHEAD, 512)
    core_copy(ROW_C3 + C3_AHEAD, 512 - C3_AHEAD, 1).start()
    emit_c4(C4_AHEAD, 1024)
    core_copy(ROW_C4 + C4_AHEAD, 1024 - C4_AHEAD, 1).start()

    def block(at):
        return grads[at : at + 16, :] + core_r[at : at + 16, :].astype(F32)

    def pack(half, places):
        for xx in range(4):
            xh, xl = xx // 2, xx % 2
            for yy in range(4):
                kind = 2 * yy + xl
                for place in range(places[0], places[0] + places[1]):
                    plane = 2 * place + half
                    r = 2 * plane + xh
                    if kind < 4:
                        val = block(144 * plane + 80 * xh + 16 * kind)
                    elif kind == 4:
                        split = block(144 * plane + 64)
                        val = jnp.concatenate([split[8 * xh : 8 * xh + 8], bias_rows], axis=0)
                    elif kind == 5:
                        val = block(ROW_C3 + 16 * r)
                    else:
                        val = block(ROW_C4 + 32 * r + 16 * (kind - 6))
                    if half:
                        by[yy, place, xx] = val.astype(BF16)
                    else:
                        bx[xx, place, yy] = val.astype(BF16)

    def arrived(ref, sem):
        pltpu.make_async_copy(ref, ref, sem).wait()

    def send_first(src, at, dst, places, axis, group):
        blocks = pl.ds(*places)
        for d in (2, 1, 3):
            pltpu.make_async_remote_copy(
                src_ref=src.at[lax.rem(at + d, 4), blocks], dst_ref=dst.at[d - 1, blocks],
                send_sem=s1_ss.at[axis], recv_sem=s1_rs.at[3 * axis + group],
                device_id=(x_dev, y_dev)[axis][d - 1], device_id_type=MESH,
            ).start()

    def send_second(src, at, dst, places, axis, group):
        blocks = pl.ds(*places)
        for d in (2, 1, 3):
            pltpu.make_async_remote_copy(
                src_ref=src.at[lax.rem(at + d, 4), blocks], dst_ref=dst.at[d - 1, blocks],
                send_sem=s2_ss.at[axis], recv_sem=s2_rs.at[3 * axis + group],
                device_id=(x_dev, y_dev)[axis][d - 1], device_id_type=MESH,
            ).start()

    def add_first(src, at, got, out, places, axis, group):
        arrived(got.at[:, pl.ds(*places)], s1_rs.at[3 * axis + group])
        for k in range(places[0], places[0] + places[1]):
            acc = src[at, k].astype(F32)
            for d in range(3):
                acc = acc + got[d, k].astype(F32)
            for i in range(4):
                out[i, k] = acc[i].astype(BF16)

    def add_second(src, at, got, base, places, axis, group):
        arrived(got.at[:, pl.ds(*places)], s2_rs.at[3 * axis + group])
        lo, n = places
        acc = src[at, lo : lo + n].astype(F32)
        for d in range(3):
            acc = acc + got[d, lo : lo + n].astype(F32)
        dz[base + lo : base + lo + n] = acc.astype(BF16)

    arrived(core_r.at[pl.ds(0, ROWS_AHEAD)], core_rs.at[0])
    bias_rows = block(ROW_BIAS)[0:8]
    pack(0, AHEAD)
    send_first(bx, x, r1x, AHEAD, 0, 0)
    pack(1, AHEAD)
    send_first(by, y, r1y, AHEAD, 1, 0)

    arrived(core_r.at[pl.ds(0, ROWS - ROWS_AHEAD)], core_rs.at[1])
    for places in (NEXT, REST):
        pack(0, places)
        pack(1, places)
    t3[0:32, :] = nt(lat3[0:32], l3).astype(BF16)
    t3[224:256, :] = nt(lat3[224:256], l3).astype(BF16)
    t4[...] = nt(lat4, l4).astype(BF16)

    add_first(bx, x, r1x, cx, AHEAD, 0, 0)
    send_second(cx, y, r2x, AHEAD, 1, 0)
    add_first(by, y, r1y, cy, AHEAD, 1, 0)
    send_second(cy, x, r2y, AHEAD, 0, 0)
    send_first(bx, x, r1x, NEXT, 0, 1)
    send_first(by, y, r1y, NEXT, 1, 1)
    send_first(bx, x, r1x, REST, 0, 2)
    send_first(by, y, r1y, REST, 1, 2)

    def send_z(plane):
        d = lax.rem(plane - z + 16, 16)

        @pl.when(d != 0)
        def _():
            pltpu.make_async_remote_copy(
                src_ref=dz.at[8 * (plane % 2) + plane // 2], dst_ref=r3.at[d],
                send_sem=z_ss.at[0], recv_sem=z_rs.at[0], device_id=dev(x, y, plane, core),
                device_id_type=MESH,
            ).start()

    add_second(cx, y, r2x, 0, AHEAD, 1, 0)
    add_second(cy, x, r2y, 8, AHEAD, 0, 0)
    pl.semaphore_wait(far_sem, 2)
    for plane in range(4):
        send_z(plane)
    add_first(bx, x, r1x, cx, NEXT, 0, 1)
    send_second(cx, y, r2x, NEXT, 1, 1)
    add_first(by, y, r1y, cy, NEXT, 1, 1)
    send_second(cy, x, r2y, NEXT, 0, 1)
    add_first(bx, x, r1x, cx, REST, 0, 2)
    send_second(cx, y, r2x, REST, 1, 2)
    add_first(by, y, r1y, cy, REST, 1, 2)
    send_second(cy, x, r2y, REST, 0, 2)
    add_second(cx, y, r2x, 0, NEXT, 1, 1)
    add_second(cy, x, r2y, 8, NEXT, 0, 1)
    for plane in range(4, 8):
        send_z(plane)
    add_second(cx, y, r2x, 0, REST, 1, 2)
    add_second(cy, x, r2y, 8, REST, 0, 2)
    for plane in PLANES_REST:
        send_z(plane)

    arrived(r3.at[pl.ds(1, 15)], z_rs.at[0])
    acc = dz[8 * lax.rem(z, 2) + z // 2].astype(F32)
    for d in range(1, 16):
        acc = acc + r3[d].astype(F32)

    piece[...] = (acc * (1.0 / LOSS_SCALE)).astype(BF16)
    gath[slide] = piece[...]
    for o in SLIDE_ORDER:
        dy, dx, dc = o // 4, (o // 2) % 2, o % 2
        xl = lax.rem(x_lo + dx, 2)
        cc = lax.rem(core + dc, 2)
        pltpu.make_async_remote_copy(
            src_ref=piece, dst_ref=gath.at[slide], send_sem=ag_ss.at[0],
            recv_sem=ag_rs.at[0], device_id=dev(2 * x_hi + xl, lax.rem(y + dy, 4), z, cc),
            device_id_type=MESH,
        ).start()

    arrived(halo_s, halo_ss.at[0])
    arrived(core_s, core_ss.at[0])
    for axis in range(2):
        arrived(bx.at[pl.ds(0, 3)], s1_ss.at[axis])
        arrived(cx.at[pl.ds(0, 3)], s2_ss.at[axis])
    arrived(dz.at[pl.ds(0, 15)], z_ss.at[0])
    arrived(gath.at[pl.ds(0, 15)], ag_ss.at[0])
    arrived(gath.at[pl.ds(0, 15)], ag_rs.at[0])


def finish(t3, t4, gath, o_t3, o_t4, o_head, o_bias, o_l3, o_l4):
    row = lax.axis_index("row")
    o_t3[...] = t3[...]
    o_t4[...] = t4[...]
    odd = lax.rem(row, 2)
    halves = [gath[8 + c].astype(F32) for c in range(2)]
    for c in range(2):
        lanes = slice(128 * c, 128 * c + 128)

        @pl.when(odd == 0)
        def _():
            for blk in range(4):
                o_head[16 * blk : 16 * blk + 16, lanes] = gath[2 * blk + c].astype(F32)
            o_head[64:72, lanes] = halves[c][0:8]

        @pl.when(odd == 1)
        def _():
            o_head[0:8, lanes] = halves[c][0:8]
            for blk in range(4):
                o_head[8 + 16 * blk : 24 + 16 * blk, lanes] = gath[2 * blk + c].astype(F32)

        o_l3[:, lanes] = gath[10 + c].astype(F32)
        o_l4[0:16, lanes] = gath[12 + c].astype(F32)
        o_l4[16:32, lanes] = gath[14 + c].astype(F32)
    sums = jnp.concatenate([halves[0][8:16], halves[1][8:16]], axis=1)
    lane = lax.broadcasted_iota(jnp.int32, (8, 256), 1)
    sub = lax.broadcasted_iota(jnp.int32, (8, 256), 0)
    mine = jnp.where(lane == 8 * row + sub, sums, 0.0)
    for i in range(8):
        o_bias[i] = jnp.sum(mine[i : i + 1, :])


def local(*args):
    shapes = (
        (256, 512), (64, 1024), (256, 256), (64, 256), (256, 256), (64, 256), (256, 256),
        (64, 256), (8, 32), (4, 16), (2304, 256), (512, 256), (1024, 256),
    )
    flat = [a.reshape(s) for a, s in zip(args, shapes)]
    vm = pltpu.VMEM
    dma = pltpu.SemaphoreType.DMA
    in_vmem = pl.BlockSpec(memory_space=vm)
    anywhere = pl.BlockSpec(memory_space=pl.ANY)
    t3, t4, gath = pl.pallas_call(
        kernel,
        out_shape=(
            vm((256, 512), BF16), vm((64, 1024), BF16), vm((16, 16, 128), BF16),
        ),
        in_specs=[anywhere] * 13,
        out_specs=(in_vmem,) * 3,
        scratch_shapes=[
            vm((16, 128), BF16), vm((WIDE, 256), BF16), vm((256, 512), BF16),
            vm((64, 1024), BF16), vm((8, 32), jnp.int32), vm((4, 16), jnp.int32),
            vm((256, 256), BF16), vm((256, 64), BF16), vm((512, 256), BF16),
            vm((1024, 64), BF16), vm((2, 256, 48), BF16),
            vm((3, 320, 256), BF16), vm((3, 96, 256), BF16),
            vm((2, 48, 256), BF16), vm((2, 48, 256), BF16),
            vm((1536, 256), F32), vm((320, 256), F32), vm((512, 256), F32),
            vm((ROWS, 128), F32), vm((ROWS, 128), BF16), vm((ROWS, 128), BF16),
            vm((4, 8, 4, 16, 128), BF16), vm((4, 8, 4, 16, 128), BF16),
            vm((3, 8, 4, 16, 128), BF16), vm((3, 8, 4, 16, 128), BF16),
            vm((4, 8, 16, 128), BF16), vm((4, 8, 16, 128), BF16),
            vm((3, 8, 16, 128), BF16), vm((3, 8, 16, 128), BF16),
            vm((16, 16, 128), BF16), vm((16, 16, 128), BF16),
            dma((6,)), dma((1,)), dma((2,)), dma((1,)), dma((2,)), dma((2,)), dma((6,)),
            dma((2,)), dma((6,)), dma((1,)), dma((1,)), dma((1,)), dma((1,)),
            pltpu.SemaphoreType.REGULAR,
        ],
        compiler_params=pltpu.CompilerParams(
            collective_id=0, has_side_effects=True, vmem_limit_bytes=56 << 20
        ),
        name="pyramid_backward",
    )(*flat)
    outs = pl.pallas_call(
        finish,
        out_shape=(
            jax.ShapeDtypeStruct((256, 512), BF16),
            jax.ShapeDtypeStruct((64, 1024), BF16),
            jax.ShapeDtypeStruct((72, 256), F32),
            jax.ShapeDtypeStruct((8,), F32),
            jax.ShapeDtypeStruct((16, 256), F32),
            jax.ShapeDtypeStruct((32, 256), F32),
        ),
        in_specs=[in_vmem] * 3,
        out_specs=(
            in_vmem, in_vmem, in_vmem, pl.BlockSpec(memory_space=pltpu.SMEM), in_vmem, in_vmem,
        ),
        name="place_outputs",
    )(*[pltpu.with_memory_space_constraint(a, vm) for a in (t3, t4, gath)])
    t3, t4, head, bias, lat3, lat4 = outs
    return (t3.reshape(1, 8, 32, 512), t4.reshape(1, 4, 16, 1024), head, bias, lat3, lat4)


def solution(mesh):
    big = P("slide", "row", None, None)
    in_specs = (big,) * 8 + (P("slide", "row", None),) * 2 + (P(),) * 3
    out_specs = (big, big, P("row", None), P("row"), P("row", None), P("row", None))
    return jax.shard_map(local, mesh=mesh, in_specs=in_specs, out_specs=out_specs, check_vma=False)
```

```python
import jax
import jax.numpy as jnp
from jax import lax
from jax.experimental import pallas as pl
from jax.experimental.pallas import tpu as pltpu
from jax.sharding import PartitionSpec as P

MESH = pl.DeviceIdType.MESH
F32 = jnp.float32
BF16 = jnp.bfloat16
LOSS_SCALE = 256.0

ROW_BIAS = 2304
ROW_C3 = 2320
ROW_C4 = 2832
ROWS = 3856
NEXT, REST = (0, 2), (2, 4)
PLANE_STEPS = (
    (2, 2), (2, 1), (2, 3), (1, 2), (3, 2), (2, 0), (0, 2), (1, 1), (1, 3), (3, 1), (3, 3),
    (1, 0), (3, 0), (0, 1), (0, 3),
)
C3_AHEAD, C4_AHEAD = 128, 256
ROWS_AHEAD = 768 + 16 + C3_AHEAD + C4_AHEAD
P3, G3, P4, G4, F3, F4, HW, L3, L4, WIDE = 0, 256, 512, 576, 640, 896, 960, 3264, 3776, 4800
PLANES_REST = (15, 14, 13, 12, 11, 10, 9, 8)
SLIDE_ORDER = (11, 10, 9, 8, 7, 15, 6, 14, 5, 13, 4, 12, 3, 2, 1)


def nt(a, b):
    return lax.dot_general(a, b, (((1,), (1,)), ((), ())), preferred_element_type=F32)


def nn(a, b):
    return jnp.dot(a, b, preferred_element_type=F32)


def kernel(
    tc3_h, tc4_h, f3_h, f4_h, p3_h, p4_h, g3_h, g4_h, k3_h, k4_h, hw_h, l3_h, l4_h,
    t3, t4, gath,
    piece, wide, tc3, tc4, k3, k4,
    f3t, f4t, c3t, c4t, edge_t, dx3, dx4, halo_s, halo_r, part, back_s, early, grads,
    core_s, core_r, ahead_s, ahead_r, bx, by, r1x, r1y, cx, cy, r2x, r2y, dz, r3,
    in_sem, halo_ss, halo_rs, core_ss, core_rs, ahead_ss, ahead_rs, s1_ss, s1_rs, s2_ss, s2_rs,
    z_ss, z_rs, ag_ss, ag_rs, far_sem,
):
    slide = lax.axis_index("slide")
    row = lax.axis_index("row")
    core = lax.rem(slide, 2)
    x_lo = lax.rem(slide // 2, 2)
    y = slide // 4
    z = row // 2
    x_hi = lax.rem(row, 2)
    x = 2 * x_hi + x_lo

    def dev(xx, yy, zz, cc):
        return ((yy * 2 + lax.rem(xx, 2)) * 2 + cc, zz * 2 + xx // 2)

    sibling = (slide + 1 - 2 * core, row)
    above = (slide, lax.rem(row + 31, 32))
    below = (slide, lax.rem(row + 1, 32))
    x_dev = [dev(lax.rem(x + d, 4), y, z, core) for d in (1, 2, 3)]
    y_dev = [dev(x, lax.rem(y + d, 4), z, core) for d in (1, 2, 3)]

    def z_dev(d):
        return dev(x, y, lax.rem(z + d + 16, 16), core)

    def load(src, dst, i):
        pltpu.make_async_copy(src, dst, in_sem.at[i]).start()

    def load_wide(src, at, rows, i):
        load(src, wide.at[pl.ds(at, rows)], i)

    def loaded(ref, i):
        pltpu.make_async_copy(ref, ref, in_sem.at[i]).wait()

    barrier = pltpu.get_barrier_semaphore()
    partners = [above, below]
    partners += [z_dev(d) for d in (-4, 4, -3, 3, -2, 2, -1, 1)] + x_dev + y_dev + [sibling]
    plane_dev = [
        dev(lax.rem(x + i, 4), lax.rem(y + j, 4), z, core) for i, j in PLANE_STEPS
    ]
    partners += [who for who, (i, j) in zip(plane_dev, PLANE_STEPS) if i and j]
    load_wide(p3_h, P3, 256, 0)
    load_wide(g3_h, G3, 256, 0)
    load_wide(p4_h, P4, 64, 0)
    load_wide(g4_h, G4, 64, 0)
    load(k3_h, k3, 1)
    load(k4_h, k4, 2)
    for who in partners:
        pl.semaphore_signal(barrier, inc=1, device_id=who, device_id_type=MESH)

    loaded(wide.at[pl.ds(0, 640)], 0)
    loaded(k3, 1)
    loaded(k4, 2)
    load_wide(f3_h, F3, 256, 3)
    load_wide(f4_h, F4, 64, 3)
    load_wide(hw_h, HW, 2304, 3)
    load_wide(l3_h, L3, 512, 3)
    load_wide(l4_h, L4, 1024, 3)
    load(tc3_h, tc3, 4)
    load(tc4_h, tc4, 5)

    def delta(keep, pre, grad, height, width):
        keep_t = jnp.transpose(keep[...].astype(F32))
        cols = [jnp.broadcast_to(keep_t[:, i : i + 1], (width, 256)) for i in range(height)]
        mask = jnp.concatenate(cols, axis=0)
        cells = height * width
        live = jnp.logical_and(mask > 0.5, wide[pre : pre + cells, :].astype(F32) > 0.0)
        return jnp.where(live, wide[grad : grad + cells, :].astype(F32), 0.0)

    def put_shifted(dst, start, rows, width, val):
        col = lax.rem(lax.broadcasted_iota(jnp.int32, (rows, 256), 0), width)
        ahead = jnp.where(col == width - 1, 0.0, pltpu.roll(val, rows - 1, 0))
        behind = jnp.where(col == 0, 0.0, pltpu.roll(val, 1, 0))
        dst[0, start : start + rows, :] = ahead.astype(BF16)
        dst[1, start : start + rows, :] = val.astype(BF16)
        dst[2, start : start + rows, :] = behind.astype(BF16)

    d3 = delta(k3, P3, G3, 8, 32)
    d4 = delta(k4, P4, G4, 4, 16)
    halo_s[0, 0:32, :] = d3[0:32].astype(BF16)
    halo_s[0, 32:48, :] = d4[0:16].astype(BF16)
    halo_s[1, 0:32, :] = d3[224:256].astype(BF16)
    halo_s[1, 32:48, :] = d4[48:64].astype(BF16)

    pl.semaphore_wait(barrier, len(partners))
    for i, who in enumerate((above, below)):
        pltpu.make_async_remote_copy(
            src_ref=halo_s.at[i], dst_ref=halo_r.at[i], send_sem=halo_ss.at[0],
            recv_sem=halo_rs.at[i], device_id=who, device_id_type=MESH,
        ).start()
    for d in (-4, 4):
        pl.semaphore_signal(far_sem, inc=1, device_id=z_dev(d), device_id_type=MESH)

    put_shifted(dx3, 32, 256, 32, d3)
    put_shifted(dx4, 16, 64, 16, d4)
    for b in range(3):
        dx3[b, 0:32, :] = jnp.zeros((32, 256), BF16)
        dx3[b, 288:320, :] = jnp.zeros((32, 256), BF16)
        dx4[b, 0:16, :] = jnp.zeros((16, 256), BF16)
        dx4[b, 80:96, :] = jnp.zeros((16, 256), BF16)

    first = core == 0

    def emit(start, rows, val):
        lo, hi = val[:, :128], val[:, 128:]
        at = pl.ds(start, rows)
        grads[at, :] = jnp.where(first, lo, hi)
        core_s[at, :] = jnp.where(first, hi, lo).astype(BF16)

    def core_copy(start, rows, i):
        at = pl.ds(start, rows)
        return pltpu.make_async_remote_copy(
            src_ref=core_s.at[at], dst_ref=core_r.at[at], send_sem=core_ss.at[0],
            recv_sem=core_rs.at[i], device_id=sibling, device_id_type=MESH,
        )

    ones = jnp.ones((16, 256), BF16)
    bias = nn(ones, dx3[1, 32:288, :]) + nn(ones[:, :64], dx4[1, 16:80, :])
    emit(ROW_BIAS, 16, bias)
    loaded(wide.at[pl.ds(F3, WIDE - F3)], 3)
    f3t[...] = jnp.transpose(wide[F3 : F3 + 256, :])
    f4t[...] = jnp.transpose(wide[F4 : F4 + 64, :])
    for i, (at3, at4) in enumerate(((F3, F4), (F3 + 224, F4 + 48))):
        edge = jnp.concatenate([wide[at3 : at3 + 32, :], wide[at4 : at4 + 16, :]], axis=0)
        edge_t[i] = jnp.transpose(edge)

    def tap_term(a, b):
        top3, top4 = (2 - a) * 32, (2 - a) * 16
        val = nn(f3t[...], dx3[b, top3 : top3 + 256, :])
        return val + nn(f4t[...], dx4[b, top4 : top4 + 64, :])

    for b in range(3):
        emit((3 + b) * 256, 256, tap_term(1, b))
    core_copy(768, 768, 1).start()
    back = jnp.zeros((320, 256), F32)
    for a in range(3):
        for b in range(3):
            top3, top4 = (2 - a) * 32, (2 - a) * 16
            patch = jnp.concatenate(
                [dx3[b, top3 : top3 + 256, :], dx4[b, top4 : top4 + 64, :]], axis=0
            )
            at = HW + 256 * (3 * a + b)
            back = back + nt(patch, wide[at : at + 256, :])
    back_s[...] = back
    for b in range(3):
        part[b * 256 : b * 256 + 256, :] = tap_term(0, b)
        part[768 + b * 256 : 1024 + b * 256, :] = tap_term(2, b)
    loaded(tc3, 4)
    loaded(tc4, 5)
    c3t[...] = jnp.transpose(tc3[...])
    c4t[...] = jnp.transpose(tc4[...])
    inner = back_s[32:224, :].astype(BF16)
    early[...] = nn(c3t[:, 32:224], inner)
    l3, l4 = wide[L3 : L3 + 512, :], wide[L4 : L4 + 1024, :]
    t3[32:224, :] = nt(inner, l3).astype(BF16)

    def edge_side(side):
        pltpu.make_async_remote_copy(
            src_ref=halo_s.at[side], dst_ref=halo_r.at[side], send_sem=halo_ss.at[0],
            recv_sem=halo_rs.at[side], device_id=above, device_id_type=MESH,
        ).wait_recv()
        valid = row > 0 if side else row < 31
        val = jnp.where(valid, halo_r[side].astype(F32), 0.0)
        i = lax.broadcasted_iota(jnp.int32, (48, 256), 0)
        last = jnp.logical_or(i == 31, i == 47)
        start = jnp.logical_or(i == 0, i == 32)
        ahead = jnp.where(last, 0.0, pltpu.roll(val, 47, 0))
        behind = jnp.where(start, 0.0, pltpu.roll(val, 1, 0))
        return [v.astype(BF16) for v in (ahead, val, behind)]

    def edge_back(side, shifted):
        add = jnp.zeros((48, 256), F32)
        for b in range(3):
            at = HW + 1536 * side + 256 * b
            add = add + nt(shifted[b], wide[at : at + 256, :])
        at3, at4 = 224 * (1 - side), 256 + 48 * (1 - side)
        back_s[at3 : at3 + 32, :] += add[0:32]
        back_s[at4 : at4 + 16, :] += add[32:48]

    def edge_head(side, shifted):
        for b in range(3):
            at = 768 * side + 256 * b
            val = part[at : at + 256, :] + nn(edge_t[1 - side], shifted[b])
            emit(1536 * side + 256 * b, 256, val)

    low = edge_side(0)
    edge_head(0, low)
    core_copy(0, 768, 0).start()
    edge_back(0, low)
    top = edge_side(1)
    edge_back(1, top)

    back3 = back_s[0:256, :]
    lat3 = back3.astype(BF16)
    rest = (back3 - lat3.astype(F32)).astype(BF16)
    cell4 = lax.broadcasted_iota(jnp.int32, (64, 256), 0)
    cell3 = lax.broadcasted_iota(jnp.int32, (64, 256), 1)
    home = (cell3 // 64) * 16 + lax.rem(cell3, 32) // 2
    pool = jnp.where(home == cell4, 1.0, 0.0).astype(BF16)
    pooled = nn(pool, lat3) + nn(pool, rest)
    lat4 = (back_s[256:320, :] + pooled).astype(BF16)

    def emit_c3(lo, hi):
        val = early[lo:hi, :] + nn(c3t[lo:hi, 0:32], lat3[0:32])
        val = val + nn(c3t[lo:hi, 224:256], lat3[224:256])
        emit(ROW_C3 + lo, hi - lo, val)

    def emit_c4(lo, hi):
        emit(ROW_C4 + lo, hi - lo, nn(c4t[lo:hi, :], lat4))

    emit_c3(0, C3_AHEAD)
    core_copy(ROW_BIAS, 16 + C3_AHEAD, 0).start()
    emit_c4(0, C4_AHEAD)
    core_copy(ROW_C4, C4_AHEAD, 0).start()
    edge_head(1, top)
    core_copy(1536, 768, 1).start()
    emit_c3(C3_AHEAD, 512)
    core_copy(ROW_C3 + C3_AHEAD, 512 - C3_AHEAD, 1).start()
    emit_c4(C4_AHEAD, 1024)
    core_copy(ROW_C4 + C4_AHEAD, 1024 - C4_AHEAD, 1).start()

    def block(at):
        return grads[at : at + 16, :] + core_r[at : at + 16, :].astype(F32)

    def placed(xx, yy, plane):
        xh, xl = xx // 2, xx % 2
        kind, r = 2 * yy + xl, 2 * plane + xh
        if kind < 4:
            val = block(144 * plane + 80 * xh + 16 * kind)
        elif kind == 4:
            split = block(144 * plane + 64)
            val = jnp.concatenate([split[8 * xh : 8 * xh + 8], bias_rows], axis=0)
        elif kind == 5:
            val = block(ROW_C3 + 16 * r)
        else:
            val = block(ROW_C4 + 32 * r + 16 * (kind - 6))
        return val.astype(BF16)

    def pack(places):
        for xx in range(4):
            for yy in range(4):
                for place in range(places[0], places[0] + places[1]):
                    bx[xx, place, yy] = placed(xx, yy, 2 * place + 4)
                    by[yy, place, xx] = placed(xx, yy, 2 * place + 5)

    def arrived(ref, sem):
        pltpu.make_async_copy(ref, ref, sem).wait()

    def send_first(src, at, dst, places, axis, group):
        blocks = pl.ds(*places)
        for d in (2, 1, 3):
            pltpu.make_async_remote_copy(
                src_ref=src.at[lax.rem(at + d, 4), blocks], dst_ref=dst.at[d - 1, blocks],
                send_sem=s1_ss.at[axis], recv_sem=s1_rs.at[2 * axis + group],
                device_id=(x_dev, y_dev)[axis][d - 1], device_id_type=MESH,
            ).start()

    def send_second(src, at, dst, places, axis, group):
        blocks = pl.ds(*places)
        for d in (2, 1, 3):
            pltpu.make_async_remote_copy(
                src_ref=src.at[lax.rem(at + d, 4), blocks], dst_ref=dst.at[d - 1, blocks],
                send_sem=s2_ss.at[axis], recv_sem=s2_rs.at[2 * axis + group],
                device_id=(x_dev, y_dev)[axis][d - 1], device_id_type=MESH,
            ).start()

    def add_first(src, at, got, out, places, axis, group):
        arrived(got.at[:, pl.ds(*places)], s1_rs.at[2 * axis + group])
        for k in range(places[0], places[0] + places[1]):
            acc = src[at, k].astype(F32)
            for d in range(3):
                acc = acc + got[d, k].astype(F32)
            for i in range(4):
                out[i, k] = acc[i].astype(BF16)

    def add_second(src, at, got, base, places, axis, group):
        arrived(got.at[:, pl.ds(*places)], s2_rs.at[2 * axis + group])
        lo, n = places
        acc = src[at, lo : lo + n].astype(F32)
        for d in range(3):
            acc = acc + got[d, lo : lo + n].astype(F32)
        dz[base + lo : base + lo + n] = acc.astype(BF16)

    arrived(core_r.at[pl.ds(0, ROWS_AHEAD)], core_rs.at[0])
    bias_rows = block(ROW_BIAS)[0:8]
    for xx in range(4):
        for yy in range(4):
            for plane in range(4):
                ahead_s[xx, yy, plane] = placed(xx, yy, plane)
    for i, (dx, dy) in enumerate(PLANE_STEPS):
        pltpu.make_async_remote_copy(
            src_ref=ahead_s.at[lax.rem(x + dx, 4), lax.rem(y + dy, 4)],
            dst_ref=ahead_r.at[i], send_sem=ahead_ss.at[0], recv_sem=ahead_rs.at[0],
            device_id=plane_dev[i], device_id_type=MESH,
        ).start()

    arrived(core_r.at[pl.ds(0, ROWS - ROWS_AHEAD)], core_rs.at[1])
    for places in (NEXT, REST):
        pack(places)
    t3[0:32, :] = nt(lat3[0:32], l3).astype(BF16)
    t3[224:256, :] = nt(lat3[224:256], l3).astype(BF16)
    t4[...] = nt(lat4, l4).astype(BF16)

    send_first(bx, x, r1x, NEXT, 0, 0)
    send_first(by, y, r1y, NEXT, 1, 0)
    send_first(bx, x, r1x, REST, 0, 1)
    send_first(by, y, r1y, REST, 1, 1)

    def slot(plane):
        return plane if plane < 4 else 4 + 6 * (plane % 2) + (plane - 4) // 2

    def send_z(plane):
        d = lax.rem(plane - z + 16, 16)

        @pl.when(d != 0)
        def _():
            pltpu.make_async_remote_copy(
                src_ref=dz.at[slot(plane)], dst_ref=r3.at[d],
                send_sem=z_ss.at[0], recv_sem=z_rs.at[0], device_id=dev(x, y, plane, core),
                device_id_type=MESH,
            ).start()

    arrived(ahead_r, ahead_rs.at[0])
    for plane in range(4):
        acc = ahead_s[x, y, plane].astype(F32)
        for i in range(15):
            acc = acc + ahead_r[i, plane].astype(F32)
        dz[plane] = acc.astype(BF16)
    pl.semaphore_wait(far_sem, 2)
    for plane in range(4):
        send_z(plane)
    add_first(bx, x, r1x, cx, NEXT, 0, 0)
    send_second(cx, y, r2x, NEXT, 1, 0)
    add_first(by, y, r1y, cy, NEXT, 1, 0)
    send_second(cy, x, r2y, NEXT, 0, 0)
    add_first(bx, x, r1x, cx, REST, 0, 1)
    send_second(cx, y, r2x, REST, 1, 1)
    add_first(by, y, r1y, cy, REST, 1, 1)
    send_second(cy, x, r2y, REST, 0, 1)
    add_second(cx, y, r2x, 4, NEXT, 1, 0)
    add_second(cy, x, r2y, 10, NEXT, 0, 0)
    for plane in range(4, 8):
        send_z(plane)
    def finish_plane():
        arrived(r3.at[pl.ds(1, 15)], z_rs.at[0])
        high = (z + 12) // 16
        home = (1 - high) * z + high * (4 + 6 * lax.rem(z, 2) + (z + 12) // 2 - 8)
        acc = dz[home].astype(F32)
        for d in range(1, 16):
            acc = acc + r3[d].astype(F32)

        piece[...] = (acc * (1.0 / LOSS_SCALE)).astype(BF16)
        gath[slide] = piece[...]
        for o in SLIDE_ORDER:
            dy, dx, dc = o // 4, (o // 2) % 2, o % 2
            xl = lax.rem(x_lo + dx, 2)
            cc = lax.rem(core + dc, 2)
            pltpu.make_async_remote_copy(
                src_ref=piece, dst_ref=gath.at[slide], send_sem=ag_ss.at[0],
                recv_sem=ag_rs.at[0], device_id=dev(2 * x_hi + xl, lax.rem(y + dy, 4), z, cc),
                device_id_type=MESH,
            ).start()

    @pl.when(z < 2)
    def _():
        finish_plane()

    add_second(cx, y, r2x, 4, REST, 1, 1)
    add_second(cy, x, r2y, 10, REST, 0, 1)
    for plane in PLANES_REST:
        send_z(plane)

    @pl.when(z >= 2)
    def _():
        finish_plane()

    arrived(halo_s, halo_ss.at[0])
    arrived(core_s, core_ss.at[0])
    arrived(ahead_r, ahead_ss.at[0])
    for axis in range(2):
        arrived(bx.at[pl.ds(0, 3)], s1_ss.at[axis])
        arrived(cx.at[pl.ds(0, 3)], s2_ss.at[axis])
    arrived(dz.at[pl.ds(0, 15)], z_ss.at[0])
    arrived(gath.at[pl.ds(0, 15)], ag_ss.at[0])
    arrived(gath.at[pl.ds(0, 15)], ag_rs.at[0])


def finish(t3, t4, gath, o_t3, o_t4, o_head, o_bias, o_l3, o_l4):
    row = lax.axis_index("row")
    o_t3[...] = t3[...]
    o_t4[...] = t4[...]
    odd = lax.rem(row, 2)
    halves = [gath[8 + c].astype(F32) for c in range(2)]
    for c in range(2):
        lanes = slice(128 * c, 128 * c + 128)

        @pl.when(odd == 0)
        def _():
            for blk in range(4):
                o_head[16 * blk : 16 * blk + 16, lanes] = gath[2 * blk + c].astype(F32)
            o_head[64:72, lanes] = halves[c][0:8]

        @pl.when(odd == 1)
        def _():
            o_head[0:8, lanes] = halves[c][0:8]
            for blk in range(4):
                o_head[8 + 16 * blk : 24 + 16 * blk, lanes] = gath[2 * blk + c].astype(F32)

        o_l3[:, lanes] = gath[10 + c].astype(F32)
        o_l4[0:16, lanes] = gath[12 + c].astype(F32)
        o_l4[16:32, lanes] = gath[14 + c].astype(F32)
    sums = jnp.concatenate([halves[0][8:16], halves[1][8:16]], axis=1)
    lane = lax.broadcasted_iota(jnp.int32, (8, 256), 1)
    sub = lax.broadcasted_iota(jnp.int32, (8, 256), 0)
    mine = jnp.where(lane == 8 * row + sub, sums, 0.0)
    for i in range(8):
        o_bias[i] = jnp.sum(mine[i : i + 1, :])


def local(*args):
    shapes = (
        (256, 512), (64, 1024), (256, 256), (64, 256), (256, 256), (64, 256), (256, 256),
        (64, 256), (8, 32), (4, 16), (2304, 256), (512, 256), (1024, 256),
    )
    flat = [a.reshape(s) for a, s in zip(args, shapes)]
    vm = pltpu.VMEM
    dma = pltpu.SemaphoreType.DMA
    in_vmem = pl.BlockSpec(memory_space=vm)
    anywhere = pl.BlockSpec(memory_space=pl.ANY)
    t3, t4, gath = pl.pallas_call(
        kernel,
        out_shape=(
            vm((256, 512), BF16), vm((64, 1024), BF16), vm((16, 16, 128), BF16),
        ),
        in_specs=[anywhere] * 13,
        out_specs=(in_vmem,) * 3,
        scratch_shapes=[
            vm((16, 128), BF16), vm((WIDE, 256), BF16), vm((256, 512), BF16),
            vm((64, 1024), BF16), vm((8, 32), jnp.int32), vm((4, 16), jnp.int32),
            vm((256, 256), BF16), vm((256, 64), BF16), vm((512, 256), BF16),
            vm((1024, 64), BF16), vm((2, 256, 48), BF16),
            vm((3, 320, 256), BF16), vm((3, 96, 256), BF16),
            vm((2, 48, 256), BF16), vm((2, 48, 256), BF16),
            vm((1536, 256), F32), vm((320, 256), F32), vm((512, 256), F32),
            vm((ROWS, 128), F32), vm((ROWS, 128), BF16), vm((ROWS, 128), BF16),
            vm((4, 4, 4, 16, 128), BF16), vm((15, 4, 16, 128), BF16),
            vm((4, 6, 4, 16, 128), BF16), vm((4, 6, 4, 16, 128), BF16),
            vm((3, 6, 4, 16, 128), BF16), vm((3, 6, 4, 16, 128), BF16),
            vm((4, 6, 16, 128), BF16), vm((4, 6, 16, 128), BF16),
            vm((3, 6, 16, 128), BF16), vm((3, 6, 16, 128), BF16),
            vm((16, 16, 128), BF16), vm((16, 16, 128), BF16),
            dma((6,)), dma((1,)), dma((2,)), dma((1,)), dma((2,)), dma((1,)), dma((1,)),
            dma((2,)), dma((4,)), dma((2,)), dma((4,)), dma((1,)), dma((1,)), dma((1,)), dma((1,)),
            pltpu.SemaphoreType.REGULAR,
        ],
        compiler_params=pltpu.CompilerParams(
            collective_id=0, has_side_effects=True, vmem_limit_bytes=56 << 20
        ),
        name="pyramid_backward",
    )(*flat)
    outs = pl.pallas_call(
        finish,
        out_shape=(
            jax.ShapeDtypeStruct((256, 512), BF16),
            jax.ShapeDtypeStruct((64, 1024), BF16),
            jax.ShapeDtypeStruct((72, 256), F32),
            jax.ShapeDtypeStruct((8,), F32),
            jax.ShapeDtypeStruct((16, 256), F32),
            jax.ShapeDtypeStruct((32, 256), F32),
        ),
        in_specs=[in_vmem] * 3,
        out_specs=(
            in_vmem, in_vmem, in_vmem, pl.BlockSpec(memory_space=pltpu.SMEM), in_vmem, in_vmem,
        ),
        name="place_outputs",
    )(*[pltpu.with_memory_space_constraint(a, vm) for a in (t3, t4, gath)])
    t3, t4, head, bias, lat3, lat4 = outs
    return (t3.reshape(1, 8, 32, 512), t4.reshape(1, 4, 16, 1024), head, bias, lat3, lat4)


def solution(mesh):
    big = P("slide", "row", None, None)
    in_specs = (big,) * 8 + (P("slide", "row", None),) * 2 + (P(),) * 3
    out_specs = (big, big, P("row", None), P("row"), P("row", None), P("row", None))
    return jax.shard_map(local, mesh=mesh, in_specs=in_specs, out_specs=out_specs, check_vma=False)
```

```python
import jax
import jax.numpy as jnp
from jax import lax
from jax.experimental import pallas as pl
from jax.experimental.pallas import tpu as pltpu
from jax.sharding import PartitionSpec as P

MESH = pl.DeviceIdType.MESH
F32 = jnp.float32
BF16 = jnp.bfloat16
LOSS_SCALE = 256.0

ROW_BIAS = 2304
ROW_C3 = 2320
ROW_C4 = 2832
ROWS = 3856
NEXT, REST = (0, 2), (2, 4)
PLANE_STEPS = (
    (2, 2), (2, 1), (2, 3), (1, 2), (3, 2), (2, 0), (0, 2), (1, 1), (1, 3), (3, 1), (3, 3),
    (1, 0), (3, 0), (0, 1), (0, 3),
)
C3_AHEAD, C4_AHEAD = 128, 256
ROWS_AHEAD = 768 + 16 + C3_AHEAD + C4_AHEAD
P3, G3, P4, G4, F3, F4, HW, L3, L4, WIDE = 0, 256, 512, 576, 640, 896, 960, 3264, 3776, 4800
PLANES_REST = (15, 14, 13, 12, 11, 10, 9, 8)
SLIDE_ORDER = (11, 10, 9, 8, 7, 15, 6, 14, 5, 13, 4, 12, 3, 2, 1)


def nt(a, b):
    return lax.dot_general(a, b, (((1,), (1,)), ((), ())), preferred_element_type=F32)


def nn(a, b):
    return jnp.dot(a, b, preferred_element_type=F32)


def kernel(
    tc3_h, tc4_h, f3_h, f4_h, p3_h, p4_h, g3_h, g4_h, k3_h, k4_h, hw_h, l3_h, l4_h,
    t3, t4, gath,
    piece, wide, tc3, tc4, k3, k4,
    f3t, f4t, c3t, c4t, edge_t, dx3, dx4, halo_s, halo_r, part, back_s, early, grads,
    core_s, core_r, ahead_s, ahead_r, bx, by, r1x, r1y, cx, cy, r2x, r2y, dz, r3,
    in_sem, halo_ss, halo_rs, core_ss, core_rs, ahead_ss, ahead_rs, s1_ss, s1_rs, s2_ss, s2_rs,
    z_ss, z_rs, ag_ss, ag_rs, far_sem,
):
    slide = lax.axis_index("slide")
    row = lax.axis_index("row")
    core = lax.rem(slide, 2)
    x_lo = lax.rem(slide // 2, 2)
    y = slide // 4
    z = row // 2
    x_hi = lax.rem(row, 2)
    x = 2 * x_hi + x_lo

    def dev(xx, yy, zz, cc):
        return ((yy * 2 + lax.rem(xx, 2)) * 2 + cc, zz * 2 + xx // 2)

    sibling = (slide + 1 - 2 * core, row)
    above = (slide, lax.rem(row + 31, 32))
    below = (slide, lax.rem(row + 1, 32))
    x_dev = [dev(lax.rem(x + d, 4), y, z, core) for d in (1, 2, 3)]
    y_dev = [dev(x, lax.rem(y + d, 4), z, core) for d in (1, 2, 3)]

    def z_dev(d):
        return dev(x, y, lax.rem(z + d + 16, 16), core)

    def load(src, dst, i):
        pltpu.make_async_copy(src, dst, in_sem.at[i]).start()

    def load_wide(src, at, rows, i):
        load(src, wide.at[pl.ds(at, rows)], i)

    def loaded(ref, i):
        pltpu.make_async_copy(ref, ref, in_sem.at[i]).wait()

    barrier = pltpu.get_barrier_semaphore()
    partners = [above, below]
    partners += [z_dev(d) for d in (-4, 4, -3, 3, -2, 2, -1, 1)] + x_dev + y_dev + [sibling]
    plane_dev = [
        dev(lax.rem(x + i, 4), lax.rem(y + j, 4), z, core) for i, j in PLANE_STEPS
    ]
    partners += [who for who, (i, j) in zip(plane_dev, PLANE_STEPS) if i and j]
    load_wide(p3_h, P3, 256, 0)
    load_wide(g3_h, G3, 256, 0)
    load_wide(p4_h, P4, 64, 0)
    load_wide(g4_h, G4, 64, 0)
    load(k3_h, k3, 1)
    load(k4_h, k4, 2)
    for who in partners:
        pl.semaphore_signal(barrier, inc=1, device_id=who, device_id_type=MESH)

    loaded(wide.at[pl.ds(0, 640)], 0)
    loaded(k3, 1)
    loaded(k4, 2)
    load_wide(f3_h, F3, 256, 3)
    load_wide(f4_h, F4, 64, 3)
    load_wide(hw_h, HW, 2304, 3)
    load_wide(l3_h, L3, 512, 3)
    load_wide(l4_h, L4, 1024, 3)
    load(tc3_h, tc3, 4)
    load(tc4_h, tc4, 5)

    def delta(keep, pre, grad, height, width):
        keep_t = jnp.transpose(keep[...].astype(F32))
        cols = [jnp.broadcast_to(keep_t[:, i : i + 1], (width, 256)) for i in range(height)]
        mask = jnp.concatenate(cols, axis=0)
        cells = height * width
        live = jnp.logical_and(mask > 0.5, wide[pre : pre + cells, :].astype(F32) > 0.0)
        return jnp.where(live, wide[grad : grad + cells, :].astype(F32), 0.0)

    def put_shifted(dst, start, rows, width, val):
        col = lax.rem(lax.broadcasted_iota(jnp.int32, (rows, 256), 0), width)
        ahead = jnp.where(col == width - 1, 0.0, pltpu.roll(val, rows - 1, 0))
        behind = jnp.where(col == 0, 0.0, pltpu.roll(val, 1, 0))
        dst[0, start : start + rows, :] = ahead.astype(BF16)
        dst[1, start : start + rows, :] = val.astype(BF16)
        dst[2, start : start + rows, :] = behind.astype(BF16)

    d3 = delta(k3, P3, G3, 8, 32)
    d4 = delta(k4, P4, G4, 4, 16)
    halo_s[0, 0:32, :] = d3[0:32].astype(BF16)
    halo_s[0, 32:48, :] = d4[0:16].astype(BF16)
    halo_s[1, 0:32, :] = d3[224:256].astype(BF16)
    halo_s[1, 32:48, :] = d4[48:64].astype(BF16)

    pl.semaphore_wait(barrier, len(partners))
    for i, who in enumerate((above, below)):
        pltpu.make_async_remote_copy(
            src_ref=halo_s.at[i], dst_ref=halo_r.at[i], send_sem=halo_ss.at[0],
            recv_sem=halo_rs.at[i], device_id=who, device_id_type=MESH,
        ).start()
    for d in (-4, 4):
        pl.semaphore_signal(far_sem, inc=1, device_id=z_dev(d), device_id_type=MESH)

    put_shifted(dx3, 32, 256, 32, d3)
    put_shifted(dx4, 16, 64, 16, d4)
    for b in range(3):
        dx3[b, 0:32, :] = jnp.zeros((32, 256), BF16)
        dx3[b, 288:320, :] = jnp.zeros((32, 256), BF16)
        dx4[b, 0:16, :] = jnp.zeros((16, 256), BF16)
        dx4[b, 80:96, :] = jnp.zeros((16, 256), BF16)

    first = core == 0

    def emit(start, rows, val):
        lo, hi = val[:, :128], val[:, 128:]
        at = pl.ds(start, rows)
        grads[at, :] = jnp.where(first, lo, hi)
        core_s[at, :] = jnp.where(first, hi, lo).astype(BF16)

    def core_copy(start, rows, i):
        at = pl.ds(start, rows)
        return pltpu.make_async_remote_copy(
            src_ref=core_s.at[at], dst_ref=core_r.at[at], send_sem=core_ss.at[0],
            recv_sem=core_rs.at[i], device_id=sibling, device_id_type=MESH,
        )

    ones = jnp.ones((16, 256), BF16)
    bias = nn(ones, dx3[1, 32:288, :]) + nn(ones[:, :64], dx4[1, 16:80, :])
    emit(ROW_BIAS, 16, bias)
    loaded(wide.at[pl.ds(F3, WIDE - F3)], 3)
    f3t[...] = jnp.transpose(wide[F3 : F3 + 256, :])
    f4t[...] = jnp.transpose(wide[F4 : F4 + 64, :])
    for i, (at3, at4) in enumerate(((F3, F4), (F3 + 224, F4 + 48))):
        edge = jnp.concatenate([wide[at3 : at3 + 32, :], wide[at4 : at4 + 16, :]], axis=0)
        edge_t[i] = jnp.transpose(edge)

    def tap_term(a, b):
        top3, top4 = (2 - a) * 32, (2 - a) * 16
        val = nn(f3t[...], dx3[b, top3 : top3 + 256, :])
        return val + nn(f4t[...], dx4[b, top4 : top4 + 64, :])

    for b in range(3):
        emit((3 + b) * 256, 256, tap_term(1, b))
    core_copy(768, 768, 1).start()
    back = jnp.zeros((320, 256), F32)
    for a in range(3):
        for b in range(3):
            top3, top4 = (2 - a) * 32, (2 - a) * 16
            patch = jnp.concatenate(
                [dx3[b, top3 : top3 + 256, :], dx4[b, top4 : top4 + 64, :]], axis=0
            )
            at = HW + 256 * (3 * a + b)
            back = back + nt(patch, wide[at : at + 256, :])
    back_s[...] = back
    for b in range(3):
        part[b * 256 : b * 256 + 256, :] = tap_term(0, b)
        part[768 + b * 256 : 1024 + b * 256, :] = tap_term(2, b)
    loaded(tc3, 4)
    loaded(tc4, 5)
    c3t[...] = jnp.transpose(tc3[...])
    c4t[...] = jnp.transpose(tc4[...])
    inner = back_s[32:224, :].astype(BF16)
    early[...] = nn(c3t[:, 32:224], inner)
    l3, l4 = wide[L3 : L3 + 512, :], wide[L4 : L4 + 1024, :]
    t3[32:224, :] = nt(inner, l3).astype(BF16)

    def edge_wait(side):
        pltpu.make_async_remote_copy(
            src_ref=halo_s.at[side], dst_ref=halo_r.at[side], send_sem=halo_ss.at[0],
            recv_sem=halo_rs.at[side], device_id=above, device_id_type=MESH,
        ).wait_recv()

    def edge_rows(side):
        valid = row > 0 if side else row < 31
        val = jnp.where(valid, halo_r[side].astype(F32), 0.0)
        i = lax.broadcasted_iota(jnp.int32, (48, 256), 0)
        last = jnp.logical_or(i == 31, i == 47)
        start = jnp.logical_or(i == 0, i == 32)
        ahead = jnp.where(last, 0.0, pltpu.roll(val, 47, 0))
        behind = jnp.where(start, 0.0, pltpu.roll(val, 1, 0))
        return [v.astype(BF16) for v in (ahead, val, behind)]

    def edge_back(side, shifted):
        add = jnp.zeros((48, 256), F32)
        for b in range(3):
            at = HW + 1536 * side + 256 * b
            add = add + nt(shifted[b], wide[at : at + 256, :])
        at3, at4 = 224 * (1 - side), 256 + 48 * (1 - side)
        back_s[at3 : at3 + 32, :] += add[0:32]
        back_s[at4 : at4 + 16, :] += add[32:48]

    def edge_head(side, shifted):
        for b in range(3):
            at = 768 * side + 256 * b
            val = part[at : at + 256, :] + nn(edge_t[1 - side], shifted[b])
            emit(1536 * side + 256 * b, 256, val)

    def above_back():
        edge_wait(1)
        edge_back(1, edge_rows(1))

    @pl.when(x_hi == 1)
    def _():
        above_back()

    edge_wait(0)
    low = edge_rows(0)
    edge_head(0, low)
    core_copy(0, 768, 0).start()
    edge_back(0, low)

    @pl.when(x_hi == 0)
    def _():
        above_back()


    back3 = back_s[0:256, :]
    lat3 = back3.astype(BF16)
    rest = (back3 - lat3.astype(F32)).astype(BF16)
    cell4 = lax.broadcasted_iota(jnp.int32, (64, 256), 0)
    cell3 = lax.broadcasted_iota(jnp.int32, (64, 256), 1)
    home = (cell3 // 64) * 16 + lax.rem(cell3, 32) // 2
    pool = jnp.where(home == cell4, 1.0, 0.0).astype(BF16)
    pooled = nn(pool, lat3) + nn(pool, rest)
    lat4 = (back_s[256:320, :] + pooled).astype(BF16)

    def emit_c3(lo, hi):
        val = early[lo:hi, :] + nn(c3t[lo:hi, 0:32], lat3[0:32])
        val = val + nn(c3t[lo:hi, 224:256], lat3[224:256])
        emit(ROW_C3 + lo, hi - lo, val)

    def emit_c4(lo, hi):
        emit(ROW_C4 + lo, hi - lo, nn(c4t[lo:hi, :], lat4))

    emit_c3(0, C3_AHEAD)
    core_copy(ROW_BIAS, 16 + C3_AHEAD, 0).start()
    emit_c4(0, C4_AHEAD)
    core_copy(ROW_C4, C4_AHEAD, 0).start()
    edge_head(1, edge_rows(1))
    core_copy(1536, 768, 1).start()
    emit_c3(C3_AHEAD, 512)
    core_copy(ROW_C3 + C3_AHEAD, 512 - C3_AHEAD, 1).start()
    emit_c4(C4_AHEAD, 1024)
    core_copy(ROW_C4 + C4_AHEAD, 1024 - C4_AHEAD, 1).start()

    def block(at):
        return grads[at : at + 16, :] + core_r[at : at + 16, :].astype(F32)

    def placed(xx, yy, plane):
        xh, xl = xx // 2, xx % 2
        kind, r = 2 * yy + xl, 2 * plane + xh
        if kind < 4:
            val = block(144 * plane + 80 * xh + 16 * kind)
        elif kind == 4:
            split = block(144 * plane + 64)
            val = jnp.concatenate([split[8 * xh : 8 * xh + 8], bias_rows], axis=0)
        elif kind == 5:
            val = block(ROW_C3 + 16 * r)
        else:
            val = block(ROW_C4 + 32 * r + 16 * (kind - 6))
        return val.astype(BF16)

    def pack(places):
        for xx in range(4):
            for yy in range(4):
                for place in range(places[0], places[0] + places[1]):
                    bx[xx, place, yy] = placed(xx, yy, 2 * place + 4)
                    by[yy, place, xx] = placed(xx, yy, 2 * place + 5)

    def arrived(ref, sem):
        pltpu.make_async_copy(ref, ref, sem).wait()

    def send_first(src, at, dst, places, axis, group):
        blocks = pl.ds(*places)
        for d in (2, 1, 3):
            pltpu.make_async_remote_copy(
                src_ref=src.at[lax.rem(at + d, 4), blocks], dst_ref=dst.at[d - 1, blocks],
                send_sem=s1_ss.at[axis], recv_sem=s1_rs.at[2 * axis + group],
                device_id=(x_dev, y_dev)[axis][d - 1], device_id_type=MESH,
            ).start()

    def send_second(src, at, dst, places, axis, group):
        blocks = pl.ds(*places)
        for d in (2, 1, 3):
            pltpu.make_async_remote_copy(
                src_ref=src.at[lax.rem(at + d, 4), blocks], dst_ref=dst.at[d - 1, blocks],
                send_sem=s2_ss.at[axis], recv_sem=s2_rs.at[2 * axis + group],
                device_id=(x_dev, y_dev)[axis][d - 1], device_id_type=MESH,
            ).start()

    def add_first(src, at, got, out, places, axis, group):
        arrived(got.at[:, pl.ds(*places)], s1_rs.at[2 * axis + group])
        for k in range(places[0], places[0] + places[1]):
            acc = src[at, k].astype(F32)
            for d in range(3):
                acc = acc + got[d, k].astype(F32)
            for i in range(4):
                out[i, k] = acc[i].astype(BF16)

    def add_second(src, at, got, base, places, axis, group):
        arrived(got.at[:, pl.ds(*places)], s2_rs.at[2 * axis + group])
        lo, n = places
        acc = src[at, lo : lo + n].astype(F32)
        for d in range(3):
            acc = acc + got[d, lo : lo + n].astype(F32)
        dz[base + lo : base + lo + n] = acc.astype(BF16)

    arrived(core_r.at[pl.ds(0, ROWS_AHEAD)], core_rs.at[0])
    bias_rows = block(ROW_BIAS)[0:8]
    for xx in range(4):
        for yy in range(4):
            for plane in range(4):
                ahead_s[xx, yy, plane] = placed(xx, yy, plane)
    for i, (dx, dy) in enumerate(PLANE_STEPS):
        pltpu.make_async_remote_copy(
            src_ref=ahead_s.at[lax.rem(x + dx, 4), lax.rem(y + dy, 4)],
            dst_ref=ahead_r.at[i], send_sem=ahead_ss.at[0], recv_sem=ahead_rs.at[0],
            device_id=plane_dev[i], device_id_type=MESH,
        ).start()

    arrived(core_r.at[pl.ds(0, ROWS - ROWS_AHEAD)], core_rs.at[1])
    for places in (NEXT, REST):
        pack(places)
    t3[0:32, :] = nt(lat3[0:32], l3).astype(BF16)
    t3[224:256, :] = nt(lat3[224:256], l3).astype(BF16)
    t4[...] = nt(lat4, l4).astype(BF16)

    send_first(bx, x, r1x, NEXT, 0, 0)
    send_first(by, y, r1y, NEXT, 1, 0)
    send_first(bx, x, r1x, REST, 0, 1)
    send_first(by, y, r1y, REST, 1, 1)

    def slot(plane):
        return plane if plane < 4 else 4 + 6 * (plane % 2) + (plane - 4) // 2

    def send_z(plane):
        d = lax.rem(plane - z + 16, 16)

        @pl.when(d != 0)
        def _():
            pltpu.make_async_remote_copy(
                src_ref=dz.at[slot(plane)], dst_ref=r3.at[d],
                send_sem=z_ss.at[0], recv_sem=z_rs.at[0], device_id=dev(x, y, plane, core),
                device_id_type=MESH,
            ).start()

    arrived(ahead_r, ahead_rs.at[0])
    for plane in range(4):
        acc = ahead_s[x, y, plane].astype(F32)
        for i in range(15):
            acc = acc + ahead_r[i, plane].astype(F32)
        dz[plane] = acc.astype(BF16)
    pl.semaphore_wait(far_sem, 2)
    for plane in range(4):
        send_z(plane)
    add_first(bx, x, r1x, cx, NEXT, 0, 0)
    send_second(cx, y, r2x, NEXT, 1, 0)
    add_first(by, y, r1y, cy, NEXT, 1, 0)
    send_second(cy, x, r2y, NEXT, 0, 0)
    add_first(bx, x, r1x, cx, REST, 0, 1)
    send_second(cx, y, r2x, REST, 1, 1)
    add_first(by, y, r1y, cy, REST, 1, 1)
    send_second(cy, x, r2y, REST, 0, 1)
    add_second(cx, y, r2x, 4, NEXT, 1, 0)
    add_second(cy, x, r2y, 10, NEXT, 0, 0)
    for plane in range(4, 8):
        send_z(plane)
    def finish_plane():
        arrived(r3.at[pl.ds(1, 15)], z_rs.at[0])
        high = (z + 12) // 16
        home = (1 - high) * z + high * (4 + 6 * lax.rem(z, 2) + (z + 12) // 2 - 8)
        acc = dz[home].astype(F32)
        for d in range(1, 16):
            acc = acc + r3[d].astype(F32)

        piece[...] = (acc * (1.0 / LOSS_SCALE)).astype(BF16)
        gath[slide] = piece[...]
        for o in SLIDE_ORDER:
            dy, dx, dc = o // 4, (o // 2) % 2, o % 2
            xl = lax.rem(x_lo + dx, 2)
            cc = lax.rem(core + dc, 2)
            pltpu.make_async_remote_copy(
                src_ref=piece, dst_ref=gath.at[slide], send_sem=ag_ss.at[0],
                recv_sem=ag_rs.at[0], device_id=dev(2 * x_hi + xl, lax.rem(y + dy, 4), z, cc),
                device_id_type=MESH,
            ).start()

    @pl.when(z < 4)
    def _():
        finish_plane()

    add_second(cx, y, r2x, 4, REST, 1, 1)
    add_second(cy, x, r2y, 10, REST, 0, 1)
    for plane in PLANES_REST:
        send_z(plane)

    @pl.when(z >= 4)
    def _():
        finish_plane()

    arrived(halo_s, halo_ss.at[0])
    arrived(core_s, core_ss.at[0])
    arrived(ahead_r, ahead_ss.at[0])
    for axis in range(2):
        arrived(bx.at[pl.ds(0, 3)], s1_ss.at[axis])
        arrived(cx.at[pl.ds(0, 3)], s2_ss.at[axis])
    arrived(dz.at[pl.ds(0, 15)], z_ss.at[0])
    arrived(gath.at[pl.ds(0, 15)], ag_ss.at[0])
    arrived(gath.at[pl.ds(0, 15)], ag_rs.at[0])


def finish(t3, t4, gath, o_t3, o_t4, o_head, o_bias, o_l3, o_l4):
    row = lax.axis_index("row")
    o_t3[...] = t3[...]
    o_t4[...] = t4[...]
    odd = lax.rem(row, 2)
    halves = [gath[8 + c].astype(F32) for c in range(2)]
    for c in range(2):
        lanes = slice(128 * c, 128 * c + 128)

        @pl.when(odd == 0)
        def _():
            for blk in range(4):
                o_head[16 * blk : 16 * blk + 16, lanes] = gath[2 * blk + c].astype(F32)
            o_head[64:72, lanes] = halves[c][0:8]

        @pl.when(odd == 1)
        def _():
            o_head[0:8, lanes] = halves[c][0:8]
            for blk in range(4):
                o_head[8 + 16 * blk : 24 + 16 * blk, lanes] = gath[2 * blk + c].astype(F32)

        o_l3[:, lanes] = gath[10 + c].astype(F32)
        o_l4[0:16, lanes] = gath[12 + c].astype(F32)
        o_l4[16:32, lanes] = gath[14 + c].astype(F32)
    sums = jnp.concatenate([halves[0][8:16], halves[1][8:16]], axis=1)
    lane = lax.broadcasted_iota(jnp.int32, (8, 256), 1)
    sub = lax.broadcasted_iota(jnp.int32, (8, 256), 0)
    mine = jnp.where(lane == 8 * row + sub, sums, 0.0)
    for i in range(8):
        o_bias[i] = jnp.sum(mine[i : i + 1, :])


def local(*args):
    shapes = (
        (256, 512), (64, 1024), (256, 256), (64, 256), (256, 256), (64, 256), (256, 256),
        (64, 256), (8, 32), (4, 16), (2304, 256), (512, 256), (1024, 256),
    )
    flat = [a.reshape(s) for a, s in zip(args, shapes)]
    vm = pltpu.VMEM
    dma = pltpu.SemaphoreType.DMA
    in_vmem = pl.BlockSpec(memory_space=vm)
    anywhere = pl.BlockSpec(memory_space=pl.ANY)
    t3, t4, gath = pl.pallas_call(
        kernel,
        out_shape=(
            vm((256, 512), BF16), vm((64, 1024), BF16), vm((16, 16, 128), BF16),
        ),
        in_specs=[anywhere] * 13,
        out_specs=(in_vmem,) * 3,
        scratch_shapes=[
            vm((16, 128), BF16), vm((WIDE, 256), BF16), vm((256, 512), BF16),
            vm((64, 1024), BF16), vm((8, 32), jnp.int32), vm((4, 16), jnp.int32),
            vm((256, 256), BF16), vm((256, 64), BF16), vm((512, 256), BF16),
            vm((1024, 64), BF16), vm((2, 256, 48), BF16),
            vm((3, 320, 256), BF16), vm((3, 96, 256), BF16),
            vm((2, 48, 256), BF16), vm((2, 48, 256), BF16),
            vm((1536, 256), F32), vm((320, 256), F32), vm((512, 256), F32),
            vm((ROWS, 128), F32), vm((ROWS, 128), BF16), vm((ROWS, 128), BF16),
            vm((4, 4, 4, 16, 128), BF16), vm((15, 4, 16, 128), BF16),
            vm((4, 6, 4, 16, 128), BF16), vm((4, 6, 4, 16, 128), BF16),
            vm((3, 6, 4, 16, 128), BF16), vm((3, 6, 4, 16, 128), BF16),
            vm((4, 6, 16, 128), BF16), vm((4, 6, 16, 128), BF16),
            vm((3, 6, 16, 128), BF16), vm((3, 6, 16, 128), BF16),
            vm((16, 16, 128), BF16), vm((16, 16, 128), BF16),
            dma((6,)), dma((1,)), dma((2,)), dma((1,)), dma((2,)), dma((1,)), dma((1,)),
            dma((2,)), dma((4,)), dma((2,)), dma((4,)), dma((1,)), dma((1,)), dma((1,)), dma((1,)),
            pltpu.SemaphoreType.REGULAR,
        ],
        compiler_params=pltpu.CompilerParams(
            collective_id=0, has_side_effects=True, vmem_limit_bytes=56 << 20
        ),
        name="pyramid_backward",
    )(*flat)
    outs = pl.pallas_call(
        finish,
        out_shape=(
            jax.ShapeDtypeStruct((256, 512), BF16),
            jax.ShapeDtypeStruct((64, 1024), BF16),
            jax.ShapeDtypeStruct((72, 256), F32),
            jax.ShapeDtypeStruct((8,), F32),
            jax.ShapeDtypeStruct((16, 256), F32),
            jax.ShapeDtypeStruct((32, 256), F32),
        ),
        in_specs=[in_vmem] * 3,
        out_specs=(
            in_vmem, in_vmem, in_vmem, pl.BlockSpec(memory_space=pltpu.SMEM), in_vmem, in_vmem,
        ),
        name="place_outputs",
    )(*[pltpu.with_memory_space_constraint(a, vm) for a in (t3, t4, gath)])
    t3, t4, head, bias, lat3, lat4 = outs
    return (t3.reshape(1, 8, 32, 512), t4.reshape(1, 4, 16, 1024), head, bias, lat3, lat4)


def solution(mesh):
    big = P("slide", "row", None, None)
    in_specs = (big,) * 8 + (P("slide", "row", None),) * 2 + (P(),) * 3
    out_specs = (big, big, P("row", None), P("row"), P("row", None), P("row", None))
    return jax.shard_map(local, mesh=mesh, in_specs=in_specs, out_specs=out_specs, check_vma=False)
```
